512 devices in a mesh: dp: 8 (over x, core), seq: 64 (over y, z).
Axes of the slice: x: 4, y: 4, z: 16, core: 2. Of those that a mesh axis runs over, the one named last changes fastest.
Arguments:
- query_raw: bfloat16 [8, 8192, 2560], P('dp', 'seq'), may hold values from -8 to 8
- key_raw: bfloat16 [8, 8192, 512], P('dp', 'seq'), may hold values from -8 to 8
- values: bfloat16 [8, 8192, 512], P('dp', 'seq'), may hold values from -6 to 6
- query_gain: float32 [128], replicated, may hold values from 0.5 to 5
- key_gain: float32 [128], replicated, may hold values from 0.5 to 5
- segment_ids: int32 [8, 8192], P('dp', 'seq'), may hold values from 0 to 15, never falling along the last dimension, each value on 1 to 896 neighbouring positions
- grad_attended: bfloat16 [8, 8192, 2560], P('dp', 'seq'), may hold values from -200 to 200
Outputs:
- attended: bfloat16 [8, 8192, 2560], P('dp', 'seq')
- grad_query_raw: bfloat16 [8, 8192, 2560], P('dp', 'seq')
- grad_key_raw: bfloat16 [8, 8192, 512], P('dp', 'seq')
- grad_values: bfloat16 [8, 8192, 512], P('dp', 'seq')
- grad_query_gain: float32 [128], replicated
- grad_key_gain: float32 [128], replicated
The draws below stay inside these ranges and needn't reach their ends.
Inputs may be any that keep to these rules, and one draw needn't show every extreme that they name: `segment_ids`: within each pack ids start at 0 and never fall; every transcript holds 1 to 896 positions, and one holds exactly that many.
All inputs are finite; a program needn't handle non-finite values.
Results may differ from the reference program's by a relative error of at most 0.01.
The reference program's roundings to bfloat16 on the way (of `query_norm`, `key_norm`, `weights` and `grad_scores`) count: a program that leaves them out, or rounds other values in their place, can miss the bound.
Values may be sent and summed in bfloat16 or wider, within the bound.
A program may use at most 64 MiB of HBM per device.

```python
import math
import jax
import jax.numpy as jnp
import numpy as np
from jax import lax

HEAD = 128
Q_HEADS = 20
KV_HEADS = 4
TOK_DEV = 128
SPAN = 7
KW = 512
PACK = 8192
DOCS = 16
N_DP = 8
N_SEQ = 64


def shared_rows(key):
    base_key = jax.random.fold_in(key, 0)
    shape = (N_DP, PACK, KV_HEADS * HEAD)
    return jax.random.normal(base_key, shape, jnp.float32)


def draw_key_raw(key, part):
    base = shared_rows(key)
    result = base
    return jnp.clip(result, -8.0, 8.0).astype(jnp.bfloat16)


def draw_query_raw(key, part):
    key = jax.random.fold_in(key, 12)
    noise = jax.random.normal(key, (N_DP, PACK, Q_HEADS * HEAD), jnp.float32)
    result = noise
    return jnp.clip(result, -8.0, 8.0).astype(jnp.bfloat16)


def gain_values(key, low, high):
    return jnp.exp(jax.random.uniform(key, (HEAD,), jnp.float32, math.log(low), math.log(high)))


def draw_query_gain(key, part):
    key = jax.random.fold_in(key, 21)
    return gain_values(key, 0.5, 2.0)


def draw_key_gain(key, part):
    key = jax.random.fold_in(key, 22)
    return gain_values(key, 0.5, 2.0)


def draw_grad_attended(key, part):
    key = jax.random.fold_in(key, 31)
    base_key, row_key = jax.random.split(key, 2)
    shape = (N_DP, PACK, Q_HEADS * HEAD)
    position = jnp.arange(PACK, dtype=jnp.float32) / PACK
    row_scale = jnp.exp(jax.random.uniform(row_key, (N_DP, PACK, 1), jnp.float32, 0.0, math.log(10.0)))
    row_scale = row_scale * jnp.exp(math.log(3.0) * position)[None, :, None]
    result = jax.random.normal(base_key, shape, jnp.float32)
    return jnp.clip(result * row_scale, -200.0, 200.0).astype(jnp.bfloat16)


def block_scale(rng, extent, cuts, least, top_value):
    def one(axis_at, blocks):
        steps = jax.random.uniform(jax.random.fold_in(jax.random.fold_in(rng, 6), axis_at), (blocks,), jnp.float32, least / len(cuts), top_value / len(cuts))
        return jnp.repeat(jnp.exp(steps), extent[axis_at] // blocks).reshape((-1,) + (1,) * (len(extent) - axis_at - 1))

    factor_of = one(*cuts[0])
    for cut in cuts[1:]:
        factor_of = factor_of * one(*cut)
    return factor_of


def split_up(count, total, reach, lean):
    loads = [(1 << 20) // math.isqrt(rank ** lean) + 1 for rank in range(2, count + 1)]
    surplus, holding = total - reach - (count - 1), [1] * (count - 1)
    while surplus > 0:
        candidates = [i for i in range(count - 1) if holding[i] < reach]
        pool, left = sum([loads[i] for i in candidates]), surplus
        for i in candidates:
            extra = min(reach - holding[i], max(1, left * loads[i] // pool), surplus)
            holding[i] = holding[i] + extra
            surplus = surplus - extra
    return np.array([reach] + holding)


def uneven(stream_key, count, total, bound, lean):
    if count == 2:
        one = jax.random.randint(stream_key, (), max(1, total - bound), min(bound, total - 1) + 1)
        return jnp.stack([one, total - one])
    tallies = jnp.asarray(split_up(count, total, bound, lean), jnp.int32)
    twos = (count - 1) // 2
    source_of, sink = tallies[1:1 + 2 * twos:2], tallies[2:2 + 2 * twos:2]
    room = jnp.minimum(source_of - 1, bound - sink)
    moved = jax.random.randint(jax.random.fold_in(stream_key, 1), (twos,), 0, 1 << 20) % (room + 1)
    tallies = tallies.at[1:1 + 2 * twos:2].set(source_of - moved).at[2:2 + 2 * twos:2].set(sink + moved)
    return tallies[jax.random.permutation(jax.random.fold_in(stream_key, 2), count)]


def normal_values(stream_key, dims, spread, bound, pieces=(), held_as=jnp.bfloat16):
    values = spread * jax.random.normal(stream_key, dims, jnp.float32)
    if pieces:
        values = values * block_scale(stream_key, dims, pieces, -0.22, 0.18)
    return jnp.clip(values, -bound, bound).astype(held_as)


def setup_inputs(seed: int = 0) -> dict:
    key_of = jax.random.split(jax.random.key(seed), 8)
    query_raw = draw_query_raw(jax.random.fold_in(key_of[7], 71), 0)
    key_raw = draw_key_raw(jax.random.fold_in(key_of[7], 71), 0)
    values = normal_values(key_of[2], (N_DP, PACK, KW), 1.0, 6.0, ((0, 8), (1, 64)))
    query_gain = draw_query_gain(jax.random.fold_in(key_of[7], 71), 0)
    key_gain = draw_key_gain(jax.random.fold_in(key_of[7], 71), 0)
    segment_ids = jax.vmap(lambda own: jnp.searchsorted(jnp.cumsum(uneven(own, DOCS, PACK, SPAN * TOK_DEV, 2)), jnp.arange(PACK), side="right"))(jax.random.split(key_of[5], N_DP)).reshape((N_DP, PACK)).astype(jnp.int32)
    grad_attended = draw_grad_attended(jax.random.fold_in(key_of[7], 71), 0)
    return {"query_raw": query_raw, "key_raw": key_raw, "values": values, "query_gain": query_gain, "key_gain": key_gain, "segment_ids": segment_ids, "grad_attended": grad_attended}


epsilon = 1e-06

def normalize(rows):
    inverse = lax.rsqrt(lax.optimization_barrier(jnp.mean(rows * rows, axis=-1, keepdims=True)) + epsilon)
    return (rows * inverse, inverse)

def norm_backward(grad, unit, inverse, gain):
    scaled = grad * gain
    return inverse * (scaled - unit * lax.optimization_barrier(jnp.mean(scaled * unit, axis=-1, keepdims=True)))

def visible_mask(seg_query, seg_window, tok_rows):
    query_pos = jnp.arange(tok_rows, dtype=jnp.int32)[:, None]
    key_pos = jnp.arange((SPAN + 1) * tok_rows, dtype=jnp.int32)[None, :] - SPAN * tok_rows
    return (seg_window[None, :] == seg_query[:, None]) & (key_pos <= query_pos)

def head_scores(queries, key_rows, visible):
    scaling = queries.shape[-1] ** (-0.5)
    scores = jnp.einsum('tgh,wh->tgw', queries.astype(jnp.float32), key_rows.astype(jnp.float32)) * scaling
    return jnp.where(visible[:, None, :], scores, -1e+30)

def group_forward(queries, key_rows, value_rows, visible):
    scores = head_scores(queries, key_rows, visible)
    row_max = lax.optimization_barrier(jnp.max(scores, axis=-1, keepdims=True))
    row_sum = lax.optimization_barrier(jnp.sum(jnp.exp(scores - row_max), axis=-1, keepdims=True))
    log_sum = row_max + jnp.log(row_sum)
    weights = jnp.exp(scores - log_sum).astype(jnp.bfloat16)
    output = jnp.einsum('tgw,wh->tgh', weights.astype(jnp.float32), value_rows.astype(jnp.float32))
    return (output, log_sum[..., 0])

def group_backward(queries, key_rows, value_rows, visible, log_sum, grad_out, correction):
    scaling = queries.shape[-1] ** (-0.5)
    scores = head_scores(queries, key_rows, visible)
    probs = jnp.exp(scores - log_sum[..., None])
    weights = probs.astype(jnp.bfloat16)
    grad_prob = jnp.einsum('tgh,wh->tgw', grad_out.astype(jnp.float32), value_rows.astype(jnp.float32))
    grad_scores = (probs * (grad_prob - correction[..., None]) * scaling).astype(jnp.bfloat16)
    grad_query = jnp.einsum('tgw,wh->tgh', grad_scores.astype(jnp.float32), key_rows.astype(jnp.float32))
    grad_key = jnp.einsum('tgw,tgh->wh', grad_scores.astype(jnp.float32), queries.astype(jnp.float32))
    grad_value = jnp.einsum('tgw,tgh->wh', weights.astype(jnp.float32), grad_out.astype(jnp.float32))
    return (grad_query, grad_key, grad_value)

def device_block(query_norm, seg_query, key_window, value_window, seg_window, grad_out):
    tok_rows = query_norm.shape[0]
    visible = visible_mask(seg_query, seg_window, tok_rows)
    query_heads = jnp.moveaxis(query_norm, 1, 0)
    key_heads = jnp.moveaxis(key_window, 1, 0)
    value_heads = jnp.moveaxis(value_window, 1, 0)

    def forward_one(operands):
        return group_forward(operands[0], operands[1], operands[2], visible)
    output, log_sum = lax.map(forward_one, (query_heads, key_heads, value_heads))
    attended = jnp.moveaxis(output, 0, 1).astype(jnp.bfloat16)
    correction = lax.optimization_barrier(jnp.sum(grad_out.astype(jnp.float32) * attended.astype(jnp.float32), axis=-1))
    grad_heads = jnp.moveaxis(grad_out, 1, 0)
    correction_heads = jnp.moveaxis(correction, 1, 0)

    def backward_one(operands):
        return group_backward(operands[0], operands[1], operands[2], visible, operands[3], operands[4], operands[5])
    grad_query, grad_key, grad_value = lax.map(backward_one, (query_heads, key_heads, value_heads, log_sum, grad_heads, correction_heads))
    return (attended, jnp.moveaxis(grad_query, 0, 1), jnp.moveaxis(grad_key, 0, 1), jnp.moveaxis(grad_value, 0, 1))

def one_pack(query_row, key_row, value_row, seg_row, grad_row, query_gain, key_gain):
    tok_rows = TOK_DEV
    group_size = Q_HEADS // KV_HEADS
    query_unit, query_inverse = normalize(query_row.astype(jnp.float32).reshape(PACK, Q_HEADS, HEAD))
    query_norm = (query_unit * query_gain).astype(jnp.bfloat16).reshape(PACK, KV_HEADS, group_size, HEAD)
    key_unit, key_inverse = normalize(key_row.astype(jnp.float32).reshape(PACK, KV_HEADS, HEAD))
    key_norm = (key_unit * key_gain).astype(jnp.bfloat16)
    margin = SPAN * tok_rows
    key_padded = jnp.concatenate([jnp.zeros((margin, KV_HEADS, HEAD), jnp.bfloat16), key_norm], axis=0)
    value_padded = jnp.concatenate([jnp.zeros((margin, KV_HEADS, HEAD), jnp.bfloat16), value_row.reshape(PACK, KV_HEADS, HEAD)], axis=0)
    seg_padded = jnp.concatenate([jnp.full((margin,), -1, jnp.int32), seg_row.astype(jnp.int32)], axis=0)
    grad_all = grad_row.reshape(PACK, KV_HEADS, group_size, HEAD)
    window_rows = (SPAN + 1) * tok_rows

    def step(carry, block_index):
        offset = (block_index * tok_rows).astype(jnp.int32)
        key_window = lax.dynamic_slice_in_dim(key_padded, offset, window_rows, 0)
        value_window = lax.dynamic_slice_in_dim(value_padded, offset, window_rows, 0)
        seg_window = lax.dynamic_slice_in_dim(seg_padded, offset, window_rows, 0)
        query_block = lax.dynamic_slice_in_dim(query_norm, offset, tok_rows, 0)
        seg_block = lax.dynamic_slice_in_dim(seg_row.astype(jnp.int32), offset, tok_rows, 0)
        grad_block = lax.dynamic_slice_in_dim(grad_all, offset, tok_rows, 0)
        attended, grad_query, grad_key, grad_value = device_block(query_block, seg_block, key_window, value_window, seg_window, grad_block)
        acc_key = lax.dynamic_update_slice_in_dim(carry[0], lax.dynamic_slice_in_dim(carry[0], offset, window_rows, 0) + grad_key, offset, 0)
        acc_value = lax.dynamic_update_slice_in_dim(carry[1], lax.dynamic_slice_in_dim(carry[1], offset, window_rows, 0) + grad_value, offset, 0)
        return ((acc_key, acc_value), (attended, grad_query))
    zeros_acc = jnp.zeros((margin + PACK, KV_HEADS, HEAD), jnp.float32)
    (acc_key, acc_value), (attended, grad_query) = lax.scan(step, (zeros_acc, zeros_acc), jnp.arange(N_SEQ, dtype=jnp.int32))
    grad_key_norm = acc_key[margin:]
    grad_value = acc_value[margin:]
    grad_query = grad_query.reshape(PACK, Q_HEADS, HEAD)
    grad_query_raw = norm_backward(grad_query, query_unit, query_inverse, query_gain).astype(jnp.bfloat16)
    grad_key_raw = norm_backward(grad_key_norm, key_unit, key_inverse, key_gain).astype(jnp.bfloat16)
    query_gain_part = lax.optimization_barrier(jnp.sum(grad_query * query_unit, axis=(0, 1)))
    key_gain_part = lax.optimization_barrier(jnp.sum(grad_key_norm * key_unit, axis=(0, 1)))
    return (attended.reshape(PACK, Q_HEADS * HEAD), grad_query_raw.reshape(PACK, Q_HEADS * HEAD), grad_key_raw.reshape(PACK, KV_HEADS * HEAD), grad_value.astype(jnp.bfloat16).reshape(PACK, KV_HEADS * HEAD), query_gain_part, key_gain_part)

def reference(query_raw, key_raw, values, query_gain, key_gain, segment_ids, grad_attended):

    def per_pack(operands):
        return one_pack(operands[0], operands[1], operands[2], operands[3], operands[4], query_gain, key_gain)
    results = lax.map(per_pack, (query_raw, key_raw, values, segment_ids, grad_attended))
    return (results[0], results[1], results[2], results[3], lax.optimization_barrier(jnp.sum(results[4], axis=0)), lax.optimization_barrier(jnp.sum(results[5], axis=0)))
```

```python
import math

import jax
import jax.numpy as jnp
from jax import lax
from jax.experimental import pallas as pl
from jax.experimental.pallas import tpu as pltpu
from jax.sharding import PartitionSpec as P

SPAN = 7
BLOCKS = SPAN + 1
HEAD = 128
TOK = 128
KV = 4
GROUP = 5
WIDTH = GROUP * TOK
STAGGER = 2
ROUNDS = (KV - 1) * STAGGER + 2 * SPAN + 1
EPSILON = 1e-06
SCALE = HEAD**-0.5
MESH = pl.DeviceIdType.MESH

NT = (((1,), (1,)), ((), ()))
NN = (((1,), (0,)), ((), ()))
TN = (((0,), (0,)), ((), ()))


def dot(a, b, dims):
    return lax.dot_general(a, b, dims, preferred_element_type=jnp.float32)


def normalize(rows):
    inverse = lax.rsqrt(jnp.mean(rows * rows, axis=-1, keepdims=True) + EPSILON)
    return rows * inverse, inverse


def norm_backward(grad, unit, inverse, gain):
    scaled = grad * gain
    return inverse * (scaled - unit * jnp.mean(scaled * unit, axis=-1, keepdims=True))


def lanes(head):
    return pl.ds(pl.multiple_of(head * HEAD, HEAD), HEAD)


def kernel(
    query_ref, key_ref, value_ref, query_gain_ref, key_gain_ref, segment_ref, grad_ref,
    attended_ref, grad_query_ref, grad_key_ref, grad_value_ref, gains_ref,
    window, ids, bias, query_norm, grad_rows, grad_cols, key_norm, key_unit, scores, row_max,
    weights, grad_scores, partial, outgoing, incoming,
    up_send, up_recv, id_send, id_recv, down_send, down_recv,
):
    count = lax.axis_size("seq")
    me = lax.axis_index("seq")
    dp = lax.axis_index("dp")
    after = lax.rem(me + 1, count)
    before = lax.rem(me + count - 1, count)

    barrier = pltpu.get_barrier_semaphore()
    for neighbour in (after, before):
        pl.semaphore_signal(barrier, inc=1, device_id=(dp, neighbour), device_id_type=MESH)

    def up(head, step):
        return pltpu.make_async_remote_copy(
            src_ref=window.at[head, step],
            dst_ref=window.at[head, step + 1],
            send_sem=up_send.at[head, step],
            recv_sem=up_recv.at[head, step],
            device_id=(dp, after),
            device_id_type=MESH,
        )

    def up_ids(step):
        return pltpu.make_async_remote_copy(
            src_ref=ids.at[step],
            dst_ref=ids.at[step + 1],
            send_sem=id_send.at[step],
            recv_sem=id_recv.at[step],
            device_id=(dp, after),
            device_id_type=MESH,
        )

    def down(head, step):
        return pltpu.make_async_remote_copy(
            src_ref=outgoing.at[head, step],
            dst_ref=incoming.at[head, step],
            send_sem=down_send.at[head, step],
            recv_sem=down_recv.at[head, step],
            device_id=(dp, before),
            device_id_type=MESH,
        )

    own_ids = segment_ref[...].astype(jnp.float32)
    ids[0] = jnp.broadcast_to(own_ids, (16, TOK)).astype(jnp.bfloat16)
    for head in range(KV):
        at = slice(head * HEAD, (head + 1) * HEAD)
        window[head, 0, :TOK] = key_ref[:, at]
        window[head, 0, TOK:] = value_ref[:, at]
    pl.semaphore_wait(barrier, 2)

    def prepare(head):
        group, member = head // GROUP, lax.rem(head, GROUP)
        rows = pl.ds(pl.multiple_of(member * TOK, TOK), TOK)
        unit, _ = normalize(query_ref[:, lanes(head)].astype(jnp.float32))
        query_norm[group, rows, :] = (unit * query_gain_ref[...]).astype(jnp.bfloat16)
        grad = grad_ref[:, lanes(head)]
        grad_rows[group, rows, :] = grad
        grad_cols[group, :, rows] = grad.astype(jnp.float32).T.astype(jnp.bfloat16)

    def mask_block(step):
        key_ids = jnp.broadcast_to(ids[step, 0:16, :].astype(jnp.float32)[0:1], (TOK, TOK)).T
        seen = key_ids == own_ids
        key_at = lax.broadcasted_iota(jnp.int32, (TOK, TOK), 0)
        query_at = lax.broadcasted_iota(jnp.int32, (TOK, TOK), 1)
        seen = seen & (key_at <= query_at + jnp.where(step > 0, TOK, 0))
        bias[step] = jnp.where(seen, 0.0, -1e30)

    def score_block(head, step):
        unit, _ = normalize(window[head, step, :TOK].astype(jnp.float32))
        key_unit[head, step] = unit
        keys = (unit * key_gain_ref[...]).astype(jnp.bfloat16)
        key_norm[head, step] = keys
        raw = dot(keys, query_norm[head], NT) * (SCALE * math.log2(math.e))
        block_bias = bias[step]
        for member in range(GROUP):
            at = slice(member * TOK, (member + 1) * TOK)
            part = raw[:, at] + block_bias
            scores[head, step, :, at] = part
            top = jnp.max(part.reshape(TOK // 8, 8, TOK), axis=0)
            row_max[head, :, at] = jnp.maximum(row_max[head, :, at], top)

    def head_work(head):
        top = jnp.max(row_max[head], axis=0, keepdims=True)

        def exponent(step, total):
            part = jnp.exp2(scores[head, step] - top)
            scores[head, step] = part
            return total + jnp.sum(part.reshape(TOK // 8, 8, WIDTH), axis=0)

        total = lax.fori_loop(0, BLOCKS, exponent, jnp.zeros((8, WIDTH), jnp.float32))
        inverse = 1.0 / jnp.sum(total, axis=0, keepdims=True)

        def weigh(step, _):
            weights[step] = (scores[head, step] * inverse).astype(jnp.bfloat16)
            partial[head, step, TOK:] = dot(weights[step], grad_rows[head], NN)
            return 0

        lax.fori_loop(0, BLOCKS, weigh, 0)
        value_rows = window[head, :, TOK:, :].reshape(BLOCKS * TOK, HEAD)
        output = dot(value_rows, weights[...].reshape(BLOCKS * TOK, WIDTH), TN)
        output = output.astype(jnp.bfloat16).astype(jnp.float32)
        correction = jnp.sum(output * grad_cols[head].astype(jnp.float32), axis=0, keepdims=True)
        for member in range(GROUP):
            at = slice(member * TOK, (member + 1) * TOK)
            attended_ref[:, lanes(head * GROUP + member)] = output[:, at].T.astype(jnp.bfloat16)
        scaled = inverse * SCALE

        def grad_block(step, _):
            grad_prob = dot(window[head, step, TOK:], grad_rows[head], NT)
            grad_scores[step] = (
                (scores[head, step] * scaled) * (grad_prob - correction)
            ).astype(jnp.bfloat16)
            grad_key = dot(grad_scores[step], query_norm[head], NN)
            partial[head, step, :TOK] = grad_key
            gains_ref[8:] += jnp.sum(
                (grad_key * key_unit[head, step]).reshape(TOK // 8, 8, HEAD), axis=0
            )
            return 0

        lax.fori_loop(0, BLOCKS, grad_block, 0)
        outgoing[head, 0] = partial[head, SPAN].astype(jnp.bfloat16)
        down(head, 0).start()

        key_rows = key_norm[head].reshape(BLOCKS * TOK, HEAD)
        grad_query = dot(key_rows, grad_scores[...].reshape(BLOCKS * TOK, WIDTH), TN)
        for member in range(GROUP):
            at = slice(member * TOK, (member + 1) * TOK)
            where = lanes(head * GROUP + member)
            unit, query_inverse = normalize(query_ref[:, where].astype(jnp.float32))
            grad = grad_query[:, at].T
            gains_ref[:8] += jnp.sum((grad * unit).reshape(TOK // 8, 8, HEAD), axis=0)
            grad_query_ref[:, where] = norm_backward(
                grad, unit, query_inverse, query_gain_ref[...]
            ).astype(jnp.bfloat16)

    def receive(head, step):
        @pl.when((step >= 1) & (step <= SPAN))
        def _():
            up(head, step - 1).wait_recv()

            @pl.when(head == 0)
            def _():
                up_ids(step - 1).wait_recv()

        @pl.when((step >= 0) & (step < SPAN))
        def _():
            up(head, step).start()

            @pl.when(head == 0)
            def _():
                up_ids(step).start()

        back = step - SPAN

        @pl.when((back >= 1) & (back <= SPAN))
        def _():
            down(head, back - 1).wait_recv()
            total = incoming[head, back - 1].astype(jnp.float32) + partial[head, SPAN - back]

            @pl.when(back < SPAN)
            def _():
                outgoing[head, back] = total.astype(jnp.bfloat16)
                down(head, back).start()

            @pl.when(back == SPAN)
            def _():
                at = lanes(head)
                unit, inverse = normalize(key_ref[:, at].astype(jnp.float32))
                grad_key_ref[:, at] = norm_backward(
                    total[:TOK], unit, inverse, key_gain_ref[...]
                ).astype(jnp.bfloat16)
                grad_value_ref[:, at] = total[TOK:].astype(jnp.bfloat16)

    def work(head, step):
        @pl.when(step == 0)
        def _():
            def one(member, carry):
                prepare(head * GROUP + member)
                return carry

            lax.fori_loop(0, GROUP, one, 0)

        @pl.when((step >= 0) & (step <= SPAN))
        def _():
            @pl.when(head == 0)
            def _():
                mask_block(step)

            score_block(head, step)

        @pl.when(step == SPAN)
        def _():
            head_work(head)

    row_max[...] = jnp.full(row_max.shape, -jnp.inf, jnp.float32)
    gains_ref[...] = jnp.zeros(gains_ref.shape, jnp.float32)

    def one_round(index, carry):
        def first(head, inner):
            receive(head, index - STAGGER * head)
            return inner

        def second(head, inner):
            work(head, index - STAGGER * head)
            return inner

        lax.fori_loop(0, KV, first, 0)
        lax.fori_loop(0, KV, second, 0)
        return carry

    lax.fori_loop(0, ROUNDS, one_round, 0)

    def drain(head, carry):
        def one(step, inner):
            up(head, step).wait_send()
            down(head, step).wait_send()

            @pl.when(head == 0)
            def _():
                up_ids(step).wait_send()

            return inner

        return lax.fori_loop(0, SPAN, one, carry)

    lax.fori_loop(0, KV, drain, 0)


def local(query_raw, key_raw, values, query_gain, key_gain, segment_ids, grad_attended):
    wide, narrow = (TOK, KV * GROUP * HEAD), (TOK, KV * HEAD)
    vmem = pl.BlockSpec(memory_space=pltpu.VMEM)
    dma = pltpu.SemaphoreType.DMA
    outs = pl.pallas_call(
        kernel,
        out_shape=(
            jax.ShapeDtypeStruct(wide, jnp.bfloat16),
            jax.ShapeDtypeStruct(wide, jnp.bfloat16),
            jax.ShapeDtypeStruct(narrow, jnp.bfloat16),
            jax.ShapeDtypeStruct(narrow, jnp.bfloat16),
            jax.ShapeDtypeStruct((16, HEAD), jnp.float32),
        ),
        in_specs=[vmem] * 7,
        out_specs=(vmem,) * 5,
        scratch_shapes=[
            pltpu.VMEM((KV, BLOCKS, 2 * TOK, HEAD), jnp.bfloat16),
            pltpu.VMEM((BLOCKS, 16, TOK), jnp.bfloat16),
            pltpu.VMEM((BLOCKS, TOK, TOK), jnp.float32),
            pltpu.VMEM((KV, WIDTH, HEAD), jnp.bfloat16),
            pltpu.VMEM((KV, WIDTH, HEAD), jnp.bfloat16),
            pltpu.VMEM((KV, HEAD, WIDTH), jnp.bfloat16),
            pltpu.VMEM((KV, BLOCKS, TOK, HEAD), jnp.bfloat16),
            pltpu.VMEM((KV, BLOCKS, TOK, HEAD), jnp.float32),
            pltpu.VMEM((KV, BLOCKS, TOK, WIDTH), jnp.float32),
            pltpu.VMEM((KV, 8, WIDTH), jnp.float32),
            pltpu.VMEM((BLOCKS, TOK, WIDTH), jnp.bfloat16),
            pltpu.VMEM((BLOCKS, TOK, WIDTH), jnp.bfloat16),
            pltpu.VMEM((KV, BLOCKS, 2 * TOK, HEAD), jnp.float32),
            pltpu.VMEM((KV, SPAN, 2 * TOK, HEAD), jnp.bfloat16),
            pltpu.VMEM((KV, SPAN, 2 * TOK, HEAD), jnp.bfloat16),
            dma((KV, SPAN)),
            dma((KV, SPAN)),
            dma((SPAN,)),
            dma((SPAN,)),
            dma((KV, SPAN)),
            dma((KV, SPAN)),
        ],
        compiler_params=pltpu.CompilerParams(
            collective_id=0, has_side_effects=True, vmem_limit_bytes=48 << 20
        ),
        cost_estimate=pl.CostEstimate(
            flops=2 * 6 * TOK * BLOCKS * TOK * HEAD * KV * GROUP,
            bytes_accessed=3 << 20,
            transcendentals=TOK * BLOCKS * TOK * KV * GROUP,
        ),
        name="attention",
    )(
        query_raw[0],
        key_raw[0],
        values[0],
        query_gain[None],
        key_gain[None],
        segment_ids,
        grad_attended[0],
    )
    attended, grad_query, grad_key, grad_values, gains = outs
    gains = lax.psum(jnp.sum(gains.reshape(2, 8, HEAD), axis=1), ("dp", "seq"))
    return (
        attended[None],
        grad_query[None],
        grad_key[None],
        grad_values[None],
        gains[0],
        gains[1],
    )


def solution(mesh):
    row = P("dp", "seq", None)
    return jax.shard_map(
        local,
        mesh=mesh,
        in_specs=(row, row, row, P(), P(), P("dp", "seq"), row),
        out_specs=(row, row, row, row, P(), P()),
        check_vma=False,
    )
```

```python
import math

import jax
import jax.numpy as jnp
from jax import lax
from jax.experimental import pallas as pl
from jax.experimental.pallas import tpu as pltpu
from jax.sharding import PartitionSpec as P

SPAN = 7
BLOCKS = SPAN + 1
HEAD = 128
TOK = 128
KV = 4
GROUP = 5
OFFSETS = (0, 1, 6, 7)
ROW = 16
WIDTH = GROUP * TOK
ROUNDS = OFFSETS[-1] + 2 * SPAN + 1
TAIL = OFFSETS[-1] + SPAN
SWAPS = (0, 1, 2, 4, 6, 8)
EPSILON = 1e-06
LIMIT = 60
SCALE = HEAD**-0.5
MESH = pl.DeviceIdType.MESH

NT = (((1,), (1,)), ((), ()))
NN = (((1,), (0,)), ((), ()))
TN = (((0,), (0,)), ((), ()))


def dot(a, b, dims):
    return lax.dot_general(a, b, dims, preferred_element_type=jnp.float32)


def normalize(rows):
    inverse = lax.rsqrt(jnp.mean(rows * rows, axis=-1, keepdims=True) + EPSILON)
    return rows * inverse, inverse


def norm_backward(grad, unit, inverse, gain):
    scaled = grad * gain
    return inverse * (scaled - unit * jnp.mean(scaled * unit, axis=-1, keepdims=True))


def lanes(head):
    return pl.ds(pl.multiple_of(head * HEAD, HEAD), HEAD)


def kernel(
    query_hbm, key_hbm, value_hbm, query_gain_ref, key_gain_ref, segment_ref, grad_hbm,
    attended_hbm, grad_query_hbm, grad_key_hbm, grad_value_hbm, gains_ref,
    window, ids, bias, query_norm, grad_rows, grad_cols, key_norm, key_unit, scores, row_max,
    weights, grad_scores, partial, outgoing, incoming,
    query_ref, grad_ref, attended_ref, grad_query_ref, grad_key_ref, grad_value_ref, sums, exchange,
    up_send, up_recv, id_send, id_recv, down_send, down_recv, swap_send, swap_recv, load, wide_store, narrow_store,
):
    count = lax.axis_size("seq")
    me = lax.axis_index("seq")
    dp = lax.axis_index("dp")
    after = lax.rem(me + 1, count)
    before = lax.rem(me + count - 1, count)

    place = lax.rem(me, ROW)
    sizes = (lax.axis_size("dp"), count // ROW, 4, 4)
    mine = (dp, me // ROW, lax.rem(place, 4), place // 4)

    def peer(phase, at):
        if phase == 0:
            return at, me
        return dp, me + (at - mine[phase]) * (0, ROW, 1, 4)[phase]

    loads = []
    for head in range(KV):
        at = slice(head * HEAD, (head + 1) * HEAD)
        loads.append((key_hbm.at[:, at], window.at[head, 0, pl.ds(0, TOK)]))
        loads.append((value_hbm.at[:, at], window.at[head, 0, pl.ds(TOK, TOK)]))
    loads.append((query_hbm, query_ref))
    loads.append((grad_hbm, grad_ref))
    loads = [pltpu.make_async_copy(a, b, load.at[i]) for i, (a, b) in enumerate(loads)]
    for copy in loads:
        copy.start()

    barrier = pltpu.get_barrier_semaphore()
    greeted = 2
    for neighbour in (after, before):
        pl.semaphore_signal(barrier, inc=1, device_id=(dp, neighbour), device_id_type=MESH)
    for phase in range(4):
        for j in range(1, sizes[phase]):
            if phase == 3 and j == 2:
                continue
            target = peer(phase, lax.rem(mine[phase] + j, sizes[phase]))
            pl.semaphore_signal(barrier, inc=1, device_id=target, device_id_type=MESH)
            greeted += 1

    def swap(phase, j, slot):
        return pltpu.make_async_remote_copy(
            src_ref=exchange.at[phase, slot],
            dst_ref=exchange.at[phase, slot],
            send_sem=swap_send.at[phase, j],
            recv_sem=swap_recv.at[phase, slot],
            device_id=peer(phase, lax.rem(mine[phase] + j, sizes[phase])),
            device_id_type=MESH,
        )

    def swap_start(phase):
        if phase == 4:
            slot = lax.rem(mine[3] + 3, 4)
            swap(3, 1, slot).start()
            return
        exchange[phase, mine[phase]] = sums[...]
        for j in range(1, sizes[phase]):
            if phase < 3 or j != 2:
                swap(phase, j, mine[phase]).start()

    def swap_finish(phase):
        if phase == 4:
            swap(3, 1, lax.rem(mine[3] + 2, 4)).wait_recv()
            swap(3, 1, lax.rem(mine[3] + 3, 4)).wait_send()
            phase = 3
        else:
            for j in range(1, sizes[phase]):
                if phase < 3 or j != 2:
                    swap(phase, j, lax.rem(mine[phase] + j, sizes[phase])).wait_recv()
                    swap(phase, j, mine[phase]).wait_send()
            if phase == 3:
                return
        total = exchange[phase, 0]
        for slot in range(1, sizes[phase]):
            total = total + exchange[phase, slot]
        sums[...] = total

    def up(head, step, part):
        rows = pl.ds(part * TOK, TOK)
        return pltpu.make_async_remote_copy(
            src_ref=window.at[head, step, rows],
            dst_ref=window.at[head, step + 1, rows],
            send_sem=up_send.at[head, step, part],
            recv_sem=up_recv.at[head, step, part],
            device_id=(dp, after),
            device_id_type=MESH,
        )

    def up_ids(step):
        return pltpu.make_async_remote_copy(
            src_ref=ids.at[step],
            dst_ref=ids.at[step + 1],
            send_sem=id_send.at[step],
            recv_sem=id_recv.at[step],
            device_id=(dp, after),
            device_id_type=MESH,
        )

    def down(head, step, part):
        rows = pl.ds(part * TOK, TOK)
        return pltpu.make_async_remote_copy(
            src_ref=outgoing.at[head, step, rows],
            dst_ref=incoming.at[head, step, rows],
            send_sem=down_send.at[head, step, part],
            recv_sem=down_recv.at[head, step, part],
            device_id=(dp, before),
            device_id_type=MESH,
        )

    own_ids = segment_ref[...].astype(jnp.float32)
    ids[0] = jnp.broadcast_to(own_ids, (16, TOK)).astype(jnp.bfloat16)
    def prepare(head):
        group, member = head // GROUP, lax.rem(head, GROUP)
        rows = pl.ds(pl.multiple_of(member * TOK, TOK), TOK)
        unit, _ = normalize(query_ref[:, lanes(head)].astype(jnp.float32))
        query_norm[group, rows, :] = (unit * query_gain_ref[...]).astype(jnp.bfloat16)
        grad = grad_ref[:, lanes(head)]
        grad_rows[group, rows, :] = grad
        grad_cols[group, :, rows] = grad.astype(jnp.float32).T.astype(jnp.bfloat16)

    def mask_block(step):
        key_ids = jnp.broadcast_to(ids[step, 0:16, :].astype(jnp.float32)[0:1], (TOK, TOK)).T
        seen = key_ids == own_ids
        key_at = lax.broadcasted_iota(jnp.int32, (TOK, TOK), 0)
        query_at = lax.broadcasted_iota(jnp.int32, (TOK, TOK), 1)
        seen = seen & (key_at <= query_at + jnp.where(step > 0, TOK, 0))
        bias[step] = jnp.where(seen, 0.0, -1e30)

    def score_block(head, step):
        unit, _ = normalize(window[head, step, :TOK].astype(jnp.float32))
        key_unit[head, step] = unit
        keys = (unit * key_gain_ref[...]).astype(jnp.bfloat16)
        key_norm[head, step] = keys
        raw = dot(keys, query_norm[head], NT) * (SCALE * math.log2(math.e))
        block_bias = bias[step]
        for member in range(GROUP):
            at = slice(member * TOK, (member + 1) * TOK)
            part = raw[:, at] + block_bias
            scores[head, step, :, at] = part
            top = jnp.max(part.reshape(TOK // 8, 8, TOK), axis=0)
            row_max[head, :, at] = jnp.maximum(row_max[head, :, at], top)

    def head_work(head):
        top = jnp.max(row_max[head], axis=0, keepdims=True)

        def exponent(step, total):
            part = jnp.exp2(scores[head, step] - top)
            scores[head, step] = part
            return total + jnp.sum(part.reshape(TOK // 8, 8, WIDTH), axis=0)

        total = lax.fori_loop(0, BLOCKS, exponent, jnp.zeros((8, WIDTH), jnp.float32))
        inverse = 1.0 / jnp.sum(total, axis=0, keepdims=True)
        rows = BLOCKS * TOK
        weights[...] = (scores[head].reshape(rows, WIDTH) * inverse).astype(jnp.bfloat16)
        partial[head, :, TOK:] = dot(weights[...], grad_rows[head], NN).reshape(BLOCKS, TOK, HEAD)
        outgoing[head, 0, TOK:] = partial[head, SPAN, TOK:].astype(jnp.bfloat16)
        down(head, 0, 1).start()
        value_rows = window[head, :, TOK:].reshape(rows, HEAD)
        output = dot(value_rows, weights[...], TN)
        output = output.astype(jnp.bfloat16).astype(jnp.float32)
        correction = jnp.sum(output * grad_cols[head].astype(jnp.float32), axis=0, keepdims=True)
        grad_prob = dot(value_rows, grad_rows[head], NT)
        grad_scores[...] = (
            scores[head].reshape(rows, WIDTH) * (inverse * SCALE) * (grad_prob - correction)
        ).astype(jnp.bfloat16)
        grad_key = dot(grad_scores[...], query_norm[head], NN)
        partial[head, :, :TOK] = grad_key.reshape(BLOCKS, TOK, HEAD)
        outgoing[head, 0, :TOK] = partial[head, SPAN, :TOK].astype(jnp.bfloat16)
        down(head, 0, 0).start()

        for member in range(GROUP):
            at = slice(member * TOK, (member + 1) * TOK)
            attended_ref[:, lanes(head * GROUP + member)] = output[:, at].T.astype(jnp.bfloat16)
        sums[8:] += jnp.sum((grad_key * key_unit[head].reshape(rows, HEAD)).reshape(-1, 8, HEAD), axis=0)
        grad_query = dot(key_norm[head].reshape(rows, HEAD), grad_scores[...], TN)
        for member in range(GROUP):
            at = slice(member * TOK, (member + 1) * TOK)
            where = lanes(head * GROUP + member)
            unit, query_inverse = normalize(query_ref[:, where].astype(jnp.float32))
            grad = grad_query[:, at].T
            sums[:8] += jnp.sum((grad * unit).reshape(TOK // 8, 8, HEAD), axis=0)
            grad_query_ref[:, where] = norm_backward(
                grad, unit, query_inverse, query_gain_ref[...]
            ).astype(jnp.bfloat16)

    def narrow(head, part):
        at = pl.ds(head * HEAD, HEAD)
        source = (grad_key_ref, grad_value_ref)[part]
        target = (grad_key_hbm, grad_value_hbm)[part]
        return pltpu.make_async_copy(
            source.at[:, at], target.at[:, at], narrow_store.at[head, part]
        )

    def wide(head, part):
        at = pl.ds(pl.multiple_of(head * GROUP * HEAD, HEAD), GROUP * HEAD)
        source = (attended_ref, grad_query_ref)[part]
        target = (attended_hbm, grad_query_hbm)[part]
        return pltpu.make_async_copy(
            source.at[:, at], target.at[:, at], wide_store.at[head, part]
        )

    def receive_up(head, step):
        @pl.when((step >= 0) & (step <= SPAN))
        def _():
            if head == 0:

                @pl.when(step > 0)
                def _():
                    up_ids(step - 1).wait_recv()

                @pl.when(step < SPAN)
                def _():
                    up_ids(step).start()

            for part in range(2):

                @pl.when(step > 0)
                def _():
                    up(head, step - 1, part).wait_recv()

                @pl.when(step < SPAN)
                def _():
                    up(head, step, part).start()

    def receive_down(head, back):
        @pl.when((back >= 1) & (back < SPAN))
        def _():
            for part in (1, 0):
                rows = slice(part * TOK, (part + 1) * TOK)
                down(head, back - 1, part).wait_recv()
                total = incoming[head, back - 1, rows].astype(jnp.float32)
                total = total + partial[head, SPAN - back, rows]
                outgoing[head, back, rows] = total.astype(jnp.bfloat16)
                down(head, back, part).start()

        @pl.when(back == SPAN)
        def _():
            at = slice(head * HEAD, (head + 1) * HEAD)
            down(head, SPAN - 1, 1).wait_recv()
            total = incoming[head, SPAN - 1, TOK:].astype(jnp.float32) + partial[head, 0, TOK:]
            grad_value_ref[:, at] = total.astype(jnp.bfloat16)
            narrow(head, 1).start()
            down(head, SPAN - 1, 0).wait_recv()
            total = incoming[head, SPAN - 1, :TOK].astype(jnp.float32) + partial[head, 0, :TOK]
            unit, inverse = normalize(window[head, 0, :TOK].astype(jnp.float32))
            grad_key_ref[:, at] = norm_backward(
                total, unit, inverse, key_gain_ref[...]
            ).astype(jnp.bfloat16)
            narrow(head, 0).start()

    def work(head, step):
        @pl.when((step >= 1) & (step <= SPAN))
        def _():
            @pl.when(head == 0)
            def _():
                mask_block(step)

            score_block(head, step)

        @pl.when(step == SPAN)
        def _():
            head_work(head)
            wide(head, 0).start()
            wide(head, 1).start()

    row_max[...] = jnp.full(row_max.shape, -jnp.inf, jnp.float32)
    sums[...] = jnp.zeros(sums.shape, jnp.float32)
    for copy in loads:
        copy.wait()

    def prepare_one(head, carry):
        prepare(head)
        return carry

    def own_one(head, carry):
        score_block(head, 0)
        return carry

    lax.fori_loop(0, KV * GROUP, prepare_one, 0)
    mask_block(0)
    lax.fori_loop(0, KV, own_one, 0)
    pl.semaphore_wait(barrier, greeted)

    def offset(head):
        return sum(
            jnp.where(head >= k, OFFSETS[k] - OFFSETS[k - 1], 0) for k in range(1, KV)
        )

    def one_round(index, carry):
        for head in range(KV):
            receive_up(head, index - OFFSETS[head])

        def second(head, inner):
            work(head, index - offset(head))
            return inner

        lax.fori_loop(0, KV, second, 0)
        for head in range(KV):
            receive_down(head, index - OFFSETS[head] - SPAN)

        for phase in range(5):

            @pl.when(index == TAIL + SWAPS[phase])
            def _():
                if phase > 0:
                    swap_finish(phase - 1)
                swap_start(phase)

        return carry

    lax.fori_loop(0, ROUNDS, one_round, 0)

    def drain(head, carry):
        def one(step, inner):
            for part in range(2):
                up(head, step, part).wait_send()
                down(head, step, part).wait_send()

            @pl.when(head == 0)
            def _():
                up_ids(step).wait_send()

            return inner

        return lax.fori_loop(0, SPAN, one, carry)

    lax.fori_loop(0, KV, drain, 0)
    for head in range(KV):
        for part in range(2):
            wide(head, part).wait()
            narrow(head, part).wait()
    swap_finish(4)
    gains_ref[...] = jnp.sum(sums[...].reshape(2, 8, HEAD), axis=1)


def deliver(*refs):
    sources, gains, targets = refs[:4], refs[4], refs[5:9]
    query_gain, key_gain = refs[9:11]
    held, loaded, stored = refs[11:15], refs[15], refs[16]
    loads, stores = [], []
    for i in range(4):
        loads.append(pltpu.make_async_copy(sources[i], held[i], loaded.at[i]))
        stores.append(pltpu.make_async_copy(held[i], targets[i], stored.at[i]))
    for copy in loads:
        copy.start()
    query_gain[...] = gains[0:1]
    key_gain[...] = gains[1:2]
    for load, store in zip(loads, stores):
        load.wait()
        store.start()
    for copy in stores:
        copy.wait()


def local(query_raw, key_raw, values, query_gain, key_gain, segment_ids, grad_attended):
    wide, narrow = (TOK, KV * GROUP * HEAD), (TOK, KV * HEAD)
    vmem = pl.BlockSpec(memory_space=pltpu.VMEM)
    hbm = pl.BlockSpec(memory_space=pltpu.HBM)
    dma = pltpu.SemaphoreType.DMA
    outs_like = (
        jax.ShapeDtypeStruct(wide, jnp.bfloat16),
        jax.ShapeDtypeStruct(wide, jnp.bfloat16),
        jax.ShapeDtypeStruct(narrow, jnp.bfloat16),
        jax.ShapeDtypeStruct(narrow, jnp.bfloat16),
        jax.ShapeDtypeStruct((2, HEAD), jnp.float32),
    )
    outs = pl.pallas_call(
        kernel,
        out_shape=outs_like,
        in_specs=[hbm, hbm, hbm, vmem, vmem, vmem, hbm],
        out_specs=(hbm,) * 4 + (vmem,),
        scratch_shapes=[
            pltpu.VMEM((KV, BLOCKS, 2 * TOK, HEAD), jnp.bfloat16),
            pltpu.VMEM((BLOCKS, 16, TOK), jnp.bfloat16),
            pltpu.VMEM((BLOCKS, TOK, TOK), jnp.float32),
            pltpu.VMEM((KV, WIDTH, HEAD), jnp.bfloat16),
            pltpu.VMEM((KV, WIDTH, HEAD), jnp.bfloat16),
            pltpu.VMEM((KV, HEAD, WIDTH), jnp.bfloat16),
            pltpu.VMEM((KV, BLOCKS, TOK, HEAD), jnp.bfloat16),
            pltpu.VMEM((KV, BLOCKS, TOK, HEAD), jnp.float32),
            pltpu.VMEM((KV, BLOCKS, TOK, WIDTH), jnp.float32),
            pltpu.VMEM((KV, 8, WIDTH), jnp.float32),
            pltpu.VMEM((BLOCKS * TOK, WIDTH), jnp.bfloat16),
            pltpu.VMEM((BLOCKS * TOK, WIDTH), jnp.bfloat16),
            pltpu.VMEM((KV, BLOCKS, 2 * TOK, HEAD), jnp.float32),
            pltpu.VMEM((KV, SPAN, 2 * TOK, HEAD), jnp.bfloat16),
            pltpu.VMEM((KV, SPAN, 2 * TOK, HEAD), jnp.bfloat16),
            pltpu.VMEM(wide, jnp.bfloat16),
            pltpu.VMEM(wide, jnp.bfloat16),
            pltpu.VMEM(wide, jnp.bfloat16),
            pltpu.VMEM(wide, jnp.bfloat16),
            pltpu.VMEM(narrow, jnp.bfloat16),
            pltpu.VMEM(narrow, jnp.bfloat16),
            pltpu.VMEM((16, HEAD), jnp.float32),
            pltpu.VMEM((4, 8, 16, HEAD), jnp.float32),
            dma((KV, SPAN, 2)),
            dma((KV, SPAN, 2)),
            dma((SPAN,)),
            dma((SPAN,)),
            dma((KV, SPAN, 2)),
            dma((KV, SPAN, 2)),
            dma((4, 8)),
            dma((4, 8)),
            dma((2 * KV + 2,)),
            dma((KV, 2)),
            dma((KV, 2)),
        ],
        compiler_params=pltpu.CompilerParams(
            collective_id=0, has_side_effects=True, vmem_limit_bytes=LIMIT << 20
        ),
        cost_estimate=pl.CostEstimate(
            flops=2 * 6 * TOK * BLOCKS * TOK * HEAD * KV * GROUP,
            bytes_accessed=3 << 20,
            transcendentals=TOK * BLOCKS * TOK * KV * GROUP,
        ),
        name="attention",
    )(
        query_raw[0],
        key_raw[0],
        values[0],
        query_gain[None],
        key_gain[None],
        segment_ids,
        grad_attended[0],
    )
    attended, grad_query, grad_key, grad_values, grad_query_gain, grad_key_gain = pl.pallas_call(
        deliver,
        out_shape=outs_like[:4] + (jax.ShapeDtypeStruct((1, HEAD), jnp.float32),) * 2,
        in_specs=[hbm] * 4 + [vmem],
        out_specs=(hbm,) * 4 + (vmem,) * 2,
        scratch_shapes=[
            pltpu.VMEM(wide, jnp.bfloat16),
            pltpu.VMEM(wide, jnp.bfloat16),
            pltpu.VMEM(narrow, jnp.bfloat16),
            pltpu.VMEM(narrow, jnp.bfloat16),
            dma((4,)),
            dma((4,)),
        ],
        name="deliver",
    )(*outs)
    return (
        attended[None],
        grad_query[None],
        grad_key[None],
        grad_values[None],
        grad_query_gain[0],
        grad_key_gain[0],
    )


def solution(mesh):
    row = P("dp", "seq", None)
    return jax.shard_map(
        local,
        mesh=mesh,
        in_specs=(row, row, row, P(), P(), P("dp", "seq"), row),
        out_specs=(row, row, row, row, P(), P()),
        check_vma=False,
    )
```

```python
import math

import jax
import jax.numpy as jnp
from jax import lax
from jax.experimental import pallas as pl
from jax.experimental.pallas import tpu as pltpu
from jax.sharding import PartitionSpec as P

SPAN = 7
BLOCKS = SPAN + 1
HEAD = 128
TOK = 128
KV = 4
GROUP = 5
OFFSETS = (0, 0, 7, 7)
ROW = 16
WIDTH = GROUP * TOK
ROUNDS = OFFSETS[-1] + 2 * SPAN + 1
TAIL = OFFSETS[-1] + SPAN
SWAPS = (0, 1, 2, 3, 5, 6)
EPSILON = 1e-06
LIMIT = 60
PIECES = 4
SCALE = HEAD**-0.5
MESH = pl.DeviceIdType.MESH

NT = (((1,), (1,)), ((), ()))
NN = (((1,), (0,)), ((), ()))
TN = (((0,), (0,)), ((), ()))


def dot(a, b, dims):
    return lax.dot_general(a, b, dims, preferred_element_type=jnp.float32)


def normalize(rows):
    inverse = lax.rsqrt(jnp.mean(rows * rows, axis=-1, keepdims=True) + EPSILON)
    return rows * inverse, inverse


def norm_backward(grad, unit, inverse, gain):
    scaled = grad * gain
    return inverse * (scaled - unit * jnp.mean(scaled * unit, axis=-1, keepdims=True))


def lanes(head):
    return pl.ds(pl.multiple_of(head * HEAD, HEAD), HEAD)


def kernel(
    query_hbm, key_hbm, value_hbm, query_gain_ref, key_gain_ref, segment_ref, grad_hbm,
    attended_hbm, grad_query_hbm, grad_key_hbm, grad_value_hbm, gains_ref,
    window, ids, bias, query_norm, grad_rows, grad_cols, key_norm, key_unit, scores, row_max,
    weights, grad_scores, partial, outgoing, incoming,
    query_ref, grad_ref, attended_ref, grad_query_ref, grad_key_ref, grad_value_ref, sums, exchange,
    up_send, up_recv, id_send, id_recv, down_send, down_recv, swap_send, swap_recv, load, wide_store, narrow_store,
):
    count = lax.axis_size("seq")
    me = lax.axis_index("seq")
    dp = lax.axis_index("dp")
    after = lax.rem(me + 1, count)
    before = lax.rem(me + count - 1, count)

    place = lax.rem(me, ROW)
    sizes = (lax.axis_size("dp"), count // ROW, 4, 4)
    mine = (dp, me // ROW, lax.rem(place, 4), place // 4)

    def peer(phase, at):
        if phase == 0:
            return at, me
        return dp, me + (at - mine[phase]) * (0, ROW, 1, 4)[phase]

    loads = []
    for head in range(KV):
        at = slice(head * HEAD, (head + 1) * HEAD)
        loads.append((key_hbm.at[:, at], window.at[head, 0, pl.ds(0, TOK)]))
        loads.append((value_hbm.at[:, at], window.at[head, 0, pl.ds(TOK, TOK)]))
    loads.append((query_hbm, query_ref))
    loads.append((grad_hbm, grad_ref))
    loads = [pltpu.make_async_copy(a, b, load.at[i]) for i, (a, b) in enumerate(loads)]
    for copy in loads:
        copy.start()

    barrier = pltpu.get_barrier_semaphore()
    greeted = 2
    for neighbour in (after, before):
        pl.semaphore_signal(barrier, inc=1, device_id=(dp, neighbour), device_id_type=MESH)
    for phase in range(4):
        for j in range(1, sizes[phase]):
            if phase == 3 and j == 2:
                continue
            target = peer(phase, lax.rem(mine[phase] + j, sizes[phase]))
            pl.semaphore_signal(barrier, inc=1, device_id=target, device_id_type=MESH)
            greeted += 1

    def swap(phase, j, slot):
        return pltpu.make_async_remote_copy(
            src_ref=exchange.at[phase, slot],
            dst_ref=exchange.at[phase, slot],
            send_sem=swap_send.at[phase, j],
            recv_sem=swap_recv.at[phase, slot],
            device_id=peer(phase, lax.rem(mine[phase] + j, sizes[phase])),
            device_id_type=MESH,
        )

    def swap_start(phase):
        if phase == 4:
            slot = lax.rem(mine[3] + 3, 4)
            swap(3, 1, slot).start()
            return
        exchange[phase, mine[phase]] = sums[...]
        for j in range(1, sizes[phase]):
            if phase < 3 or j != 2:
                swap(phase, j, mine[phase]).start()

    def swap_finish(phase):
        if phase == 4:
            swap(3, 1, lax.rem(mine[3] + 2, 4)).wait_recv()
            swap(3, 1, lax.rem(mine[3] + 3, 4)).wait_send()
            phase = 3
        else:
            for j in range(1, sizes[phase]):
                if phase < 3 or j != 2:
                    swap(phase, j, lax.rem(mine[phase] + j, sizes[phase])).wait_recv()
                    swap(phase, j, mine[phase]).wait_send()
            if phase == 3:
                return
        total = exchange[phase, 0]
        for slot in range(1, sizes[phase]):
            total = total + exchange[phase, slot]
        sums[...] = total

    def up(head, step, part):
        rows = pl.ds(part * TOK, TOK)
        return pltpu.make_async_remote_copy(
            src_ref=window.at[head, step, rows],
            dst_ref=window.at[head, step + 1, rows],
            send_sem=up_send.at[head, step, part],
            recv_sem=up_recv.at[head, step, part],
            device_id=(dp, after),
            device_id_type=MESH,
        )

    def up_ids(step):
        return pltpu.make_async_remote_copy(
            src_ref=ids.at[step],
            dst_ref=ids.at[step + 1],
            send_sem=id_send.at[step],
            recv_sem=id_recv.at[step],
            device_id=(dp, after),
            device_id_type=MESH,
        )

    def down(head, step, part):
        rows = pl.ds(part * TOK, TOK)
        return pltpu.make_async_remote_copy(
            src_ref=outgoing.at[head, step, rows],
            dst_ref=incoming.at[head, step, rows],
            send_sem=down_send.at[head, step, part],
            recv_sem=down_recv.at[head, step, part],
            device_id=(dp, before),
            device_id_type=MESH,
        )

    own_ids = segment_ref[...].astype(jnp.float32)
    ids[0] = jnp.broadcast_to(own_ids, (16, TOK)).astype(jnp.bfloat16)
    def prepare(head):
        group, member = head // GROUP, lax.rem(head, GROUP)
        rows = pl.ds(pl.multiple_of(member * TOK, TOK), TOK)
        unit, _ = normalize(query_ref[:, lanes(head)].astype(jnp.float32))
        query_norm[group, rows, :] = (unit * query_gain_ref[...]).astype(jnp.bfloat16)
        grad = grad_ref[:, lanes(head)]
        grad_rows[group, rows, :] = grad
        grad_cols[group, :, rows] = grad.astype(jnp.float32).T.astype(jnp.bfloat16)

    def mask_block(step):
        key_ids = jnp.broadcast_to(ids[step, 0:16, :].astype(jnp.float32)[0:1], (TOK, TOK)).T
        seen = key_ids == own_ids
        key_at = lax.broadcasted_iota(jnp.int32, (TOK, TOK), 0)
        query_at = lax.broadcasted_iota(jnp.int32, (TOK, TOK), 1)
        seen = seen & (key_at <= query_at + jnp.where(step > 0, TOK, 0))
        bias[step] = jnp.where(seen, 0.0, -1e30)

    def score_block(head, step):
        unit, _ = normalize(window[head, step, :TOK].astype(jnp.float32))
        key_unit[head, step] = unit
        keys = (unit * key_gain_ref[...]).astype(jnp.bfloat16)
        key_norm[head, step] = keys
        raw = dot(keys, query_norm[head], NT) * (SCALE * math.log2(math.e))
        block_bias = bias[step]
        for member in range(GROUP):
            at = slice(member * TOK, (member + 1) * TOK)
            part = raw[:, at] + block_bias
            scores[head, step, :, at] = part
            top = jnp.max(part.reshape(TOK // 8, 8, TOK), axis=0)
            row_max[head, :, at] = jnp.maximum(row_max[head, :, at], top)

    def head_work(head):
        top = jnp.max(row_max[head], axis=0, keepdims=True)

        def exponent(step, total):
            part = jnp.exp2(scores[head, step] - top)
            scores[head, step] = part
            return total + jnp.sum(part.reshape(TOK // 8, 8, WIDTH), axis=0)

        total = lax.fori_loop(0, BLOCKS, exponent, jnp.zeros((8, WIDTH), jnp.float32))
        inverse = 1.0 / jnp.sum(total, axis=0, keepdims=True)
        near, rows = SPAN * TOK, BLOCKS * TOK

        weights[near:] = (scores[head, SPAN] * inverse).astype(jnp.bfloat16)
        grad_value = dot(weights[near:], grad_rows[head], NN)
        outgoing[head, 0, TOK:] = grad_value.astype(jnp.bfloat16)
        down(head, 0, 1).start()

        weights[:near] = (scores[head, :SPAN].reshape(near, WIDTH) * inverse).astype(jnp.bfloat16)
        output = dot(window[head, :, TOK:].reshape(rows, HEAD), weights[...], TN)
        output = output.astype(jnp.bfloat16).astype(jnp.float32)
        correction = jnp.sum(output * grad_cols[head].astype(jnp.float32), axis=0, keepdims=True)
        scaled = inverse * SCALE

        grad_prob = dot(window[head, SPAN, TOK:], grad_rows[head], NT)
        grad_scores[near:] = (
            scores[head, SPAN] * scaled * (grad_prob - correction)
        ).astype(jnp.bfloat16)
        grad_key = dot(grad_scores[near:], query_norm[head], NN)
        outgoing[head, 0, :TOK] = grad_key.astype(jnp.bfloat16)
        down(head, 0, 0).start()
        sums[8:] += jnp.sum((grad_key * key_unit[head, SPAN]).reshape(-1, 8, HEAD), axis=0)

        grad_value = dot(weights[:near], grad_rows[head], NN)
        partial[head, :, TOK:] = grad_value.reshape(SPAN, TOK, HEAD)
        value_rows = window[head, :SPAN, TOK:].reshape(near, HEAD)
        grad_prob = dot(value_rows, grad_rows[head], NT)
        grad_scores[:near] = (
            scores[head, :SPAN].reshape(near, WIDTH) * scaled * (grad_prob - correction)
        ).astype(jnp.bfloat16)
        grad_key = dot(grad_scores[:near], query_norm[head], NN)
        partial[head, :, :TOK] = grad_key.reshape(SPAN, TOK, HEAD)
        units = key_unit[head, :SPAN].reshape(near, HEAD)
        sums[8:] += jnp.sum((grad_key * units).reshape(-1, 8, HEAD), axis=0)

        for member in range(GROUP):
            at = slice(member * TOK, (member + 1) * TOK)
            attended_ref[:, lanes(head * GROUP + member)] = output[:, at].T.astype(jnp.bfloat16)
        grad_query = dot(key_norm[head].reshape(rows, HEAD), grad_scores[...], TN)
        for member in range(GROUP):
            at = slice(member * TOK, (member + 1) * TOK)
            where = lanes(head * GROUP + member)
            unit, query_inverse = normalize(query_ref[:, where].astype(jnp.float32))
            grad = grad_query[:, at].T
            sums[:8] += jnp.sum((grad * unit).reshape(TOK // 8, 8, HEAD), axis=0)
            grad_query_ref[:, where] = norm_backward(
                grad, unit, query_inverse, query_gain_ref[...]
            ).astype(jnp.bfloat16)

    def narrow(head, part):
        at = pl.ds(head * HEAD, HEAD)
        source = (grad_key_ref, grad_value_ref)[part]
        target = (grad_key_hbm, grad_value_hbm)[part]
        return pltpu.make_async_copy(
            source.at[:, at], target.at[:, at], narrow_store.at[head, part]
        )

    def wide(head, part):
        at = pl.ds(pl.multiple_of(head * GROUP * HEAD, HEAD), GROUP * HEAD)
        source = (attended_ref, grad_query_ref)[part]
        target = (attended_hbm, grad_query_hbm)[part]
        return pltpu.make_async_copy(
            source.at[:, at], target.at[:, at], wide_store.at[head, part]
        )

    def receive_up(head, step):
        @pl.when((step >= 0) & (step <= SPAN))
        def _():
            if head == 0:

                @pl.when(step > 0)
                def _():
                    up_ids(step - 1).wait_recv()

                @pl.when(step < SPAN)
                def _():
                    up_ids(step).start()

            for part in range(2):

                @pl.when(step > 0)
                def _():
                    up(head, step - 1, part).wait_recv()

                @pl.when(step < SPAN)
                def _():
                    up(head, step, part).start()

    def receive_down(head, back):
        @pl.when((back >= 1) & (back < SPAN))
        def _():
            for part in (1, 0):
                rows = slice(part * TOK, (part + 1) * TOK)
                down(head, back - 1, part).wait_recv()
                total = incoming[head, back - 1, rows].astype(jnp.float32)
                total = total + partial[head, SPAN - back, rows]
                outgoing[head, back, rows] = total.astype(jnp.bfloat16)
                down(head, back, part).start()

        @pl.when(back == SPAN)
        def _():
            at = slice(head * HEAD, (head + 1) * HEAD)
            down(head, SPAN - 1, 1).wait_recv()
            total = incoming[head, SPAN - 1, TOK:].astype(jnp.float32) + partial[head, 0, TOK:]
            grad_value_ref[:, at] = total.astype(jnp.bfloat16)
            narrow(head, 1).start()
            down(head, SPAN - 1, 0).wait_recv()
            total = incoming[head, SPAN - 1, :TOK].astype(jnp.float32) + partial[head, 0, :TOK]
            unit, inverse = normalize(window[head, 0, :TOK].astype(jnp.float32))
            grad_key_ref[:, at] = norm_backward(
                total, unit, inverse, key_gain_ref[...]
            ).astype(jnp.bfloat16)
            narrow(head, 0).start()

    def work(head, step):
        @pl.when((step >= 1) & (step <= SPAN))
        def _():
            @pl.when(head == 0)
            def _():
                mask_block(step)

            score_block(head, step)

        @pl.when(step == SPAN)
        def _():
            head_work(head)
            wide(head, 0).start()
            wide(head, 1).start()

    row_max[...] = jnp.full(row_max.shape, -jnp.inf, jnp.float32)
    sums[...] = jnp.zeros(sums.shape, jnp.float32)
    for copy in loads[:-2]:
        copy.wait()
    pl.semaphore_wait(barrier, greeted)

    def ready(head):
        def one(member, carry):
            prepare(head * GROUP + member)
            return carry

        @pl.when(head == 0)
        def _():
            for copy in loads[-2:]:
                copy.wait()
            mask_block(0)

        lax.fori_loop(0, GROUP, one, 0)
        score_block(head, 0)

    def offset(head):
        return sum(
            jnp.where(head >= k, OFFSETS[k] - OFFSETS[k - 1], 0) for k in range(1, KV)
        )

    def one_round(index, carry):
        for head in range(KV):
            receive_up(head, index - OFFSETS[head])

        def second(head, inner):
            work(head, index - offset(head))
            return inner

        @pl.when(index < KV)
        def _():
            ready(index)

        lax.fori_loop(0, KV, second, 0)
        for head in range(KV):
            receive_down(head, index - OFFSETS[head] - SPAN)

        for phase in range(6):

            @pl.when(index == TAIL + SWAPS[phase])
            def _():
                if phase > 0:
                    swap_finish(phase - 1)
                if phase < 5:
                    swap_start(phase)

        return carry

    lax.fori_loop(0, ROUNDS, one_round, 0)

    def drain(head, carry):
        def one(step, inner):
            for part in range(2):
                up(head, step, part).wait_send()
                down(head, step, part).wait_send()

            @pl.when(head == 0)
            def _():
                up_ids(step).wait_send()

            return inner

        return lax.fori_loop(0, SPAN, one, carry)

    lax.fori_loop(0, KV, drain, 0)
    for head in range(KV):
        for part in range(2):
            wide(head, part).wait()
            narrow(head, part).wait()
    gains_ref[...] = jnp.sum(sums[...].reshape(2, 8, HEAD), axis=1)


def deliver(*refs):
    sources, gains, targets = refs[:4], refs[4], refs[5:9]
    query_gain, key_gain = refs[9:11]
    held, loaded, stored = refs[11:15], refs[15], refs[16]
    loads, stores = [], []
    for i in range(4):
        for j in range(PIECES):
            at = pl.ds(j * (TOK // PIECES), TOK // PIECES)
            loads.append(
                pltpu.make_async_copy(sources[i].at[at], held[i].at[at], loaded.at[i, j])
            )
            stores.append(
                pltpu.make_async_copy(held[i].at[at], targets[i].at[at], stored.at[i, j])
            )
    for copy in loads:
        copy.start()
    query_gain[...] = gains[0:1]
    key_gain[...] = gains[1:2]
    for load, store in zip(loads, stores):
        load.wait()
        store.start()
    for copy in stores:
        copy.wait()


def local(query_raw, key_raw, values, query_gain, key_gain, segment_ids, grad_attended):
    wide, narrow = (TOK, KV * GROUP * HEAD), (TOK, KV * HEAD)
    vmem = pl.BlockSpec(memory_space=pltpu.VMEM)
    hbm = pl.BlockSpec(memory_space=pltpu.HBM)
    dma = pltpu.SemaphoreType.DMA
    outs_like = (
        jax.ShapeDtypeStruct(wide, jnp.bfloat16),
        jax.ShapeDtypeStruct(wide, jnp.bfloat16),
        jax.ShapeDtypeStruct(narrow, jnp.bfloat16),
        jax.ShapeDtypeStruct(narrow, jnp.bfloat16),
        jax.ShapeDtypeStruct((2, HEAD), jnp.float32),
    )
    outs = pl.pallas_call(
        kernel,
        out_shape=outs_like,
        in_specs=[hbm, hbm, hbm, vmem, vmem, vmem, hbm],
        out_specs=(hbm,) * 4 + (vmem,),
        scratch_shapes=[
            pltpu.VMEM((KV, BLOCKS, 2 * TOK, HEAD), jnp.bfloat16),
            pltpu.VMEM((BLOCKS, 16, TOK), jnp.bfloat16),
            pltpu.VMEM((BLOCKS, TOK, TOK), jnp.float32),
            pltpu.VMEM((KV, WIDTH, HEAD), jnp.bfloat16),
            pltpu.VMEM((KV, WIDTH, HEAD), jnp.bfloat16),
            pltpu.VMEM((KV, HEAD, WIDTH), jnp.bfloat16),
            pltpu.VMEM((KV, BLOCKS, TOK, HEAD), jnp.bfloat16),
            pltpu.VMEM((KV, BLOCKS, TOK, HEAD), jnp.float32),
            pltpu.VMEM((KV, BLOCKS, TOK, WIDTH), jnp.float32),
            pltpu.VMEM((KV, 8, WIDTH), jnp.float32),
            pltpu.VMEM((BLOCKS * TOK, WIDTH), jnp.bfloat16),
            pltpu.VMEM((BLOCKS * TOK, WIDTH), jnp.bfloat16),
            pltpu.VMEM((KV, SPAN, 2 * TOK, HEAD), jnp.float32),
            pltpu.VMEM((KV, SPAN, 2 * TOK, HEAD), jnp.bfloat16),
            pltpu.VMEM((KV, SPAN, 2 * TOK, HEAD), jnp.bfloat16),
            pltpu.VMEM(wide, jnp.bfloat16),
            pltpu.VMEM(wide, jnp.bfloat16),
            pltpu.VMEM(wide, jnp.bfloat16),
            pltpu.VMEM(wide, jnp.bfloat16),
            pltpu.VMEM(narrow, jnp.bfloat16),
            pltpu.VMEM(narrow, jnp.bfloat16),
            pltpu.VMEM((16, HEAD), jnp.float32),
            pltpu.VMEM((4, 8, 16, HEAD), jnp.float32),
            dma((KV, SPAN, 2)),
            dma((KV, SPAN, 2)),
            dma((SPAN,)),
            dma((SPAN,)),
            dma((KV, SPAN, 2)),
            dma((KV, SPAN, 2)),
            dma((4, 8)),
            dma((4, 8)),
            dma((2 * KV + 2,)),
            dma((KV, 2)),
            dma((KV, 2)),
        ],
        compiler_params=pltpu.CompilerParams(
            collective_id=0, has_side_effects=True, vmem_limit_bytes=LIMIT << 20
        ),
        cost_estimate=pl.CostEstimate(
            flops=2 * 6 * TOK * BLOCKS * TOK * HEAD * KV * GROUP,
            bytes_accessed=3 << 20,
            transcendentals=TOK * BLOCKS * TOK * KV * GROUP,
        ),
        name="attention",
    )(
        query_raw[0],
        key_raw[0],
        values[0],
        query_gain[None],
        key_gain[None],
        segment_ids,
        grad_attended[0],
    )
    attended, grad_query, grad_key, grad_values, grad_query_gain, grad_key_gain = pl.pallas_call(
        deliver,
        out_shape=outs_like[:4] + (jax.ShapeDtypeStruct((1, HEAD), jnp.float32),) * 2,
        in_specs=[hbm] * 4 + [vmem],
        out_specs=(hbm,) * 4 + (vmem,) * 2,
        scratch_shapes=[
            pltpu.VMEM(wide, jnp.bfloat16),
            pltpu.VMEM(wide, jnp.bfloat16),
            pltpu.VMEM(narrow, jnp.bfloat16),
            pltpu.VMEM(narrow, jnp.bfloat16),
            dma((4, PIECES)),
            dma((4, PIECES)),
        ],
        name="deliver",
    )(*outs)
    return (
        attended[None],
        grad_query[None],
        grad_key[None],
        grad_values[None],
        grad_query_gain[0],
        grad_key_gain[0],
    )


def solution(mesh):
    row = P("dp", "seq", None)
    return jax.shard_map(
        local,
        mesh=mesh,
        in_specs=(row, row, row, P(), P(), P("dp", "seq"), row),
        out_specs=(row, row, row, row, P(), P()),
        check_vma=False,
    )
```

```python
import math

import jax
import jax.numpy as jnp
from jax import lax
from jax.experimental import pallas as pl
from jax.experimental.pallas import tpu as pltpu
from jax.sharding import PartitionSpec as P

SPAN = 7
BLOCKS = SPAN + 1
HEAD = 128
TOK = 128
KV = 4
GROUP = 5
OFFSETS = (0, 0, 7, 7)
LATE = (1, 1, 0, 0)
ROW = 16
WIDTH = GROUP * TOK
ROUNDS = OFFSETS[-1] + 2 * SPAN + 1
TAIL = OFFSETS[-1] + SPAN
SWAPS = (0, 1, 2, 3, 5, 6)
EPSILON = 1e-06
LIMIT = 60
SCALE = HEAD**-0.5
MESH = pl.DeviceIdType.MESH

NT = (((1,), (1,)), ((), ()))
NN = (((1,), (0,)), ((), ()))
TN = (((0,), (0,)), ((), ()))


def dot(a, b, dims):
    return lax.dot_general(a, b, dims, preferred_element_type=jnp.float32)


def normalize(rows):
    inverse = lax.rsqrt(jnp.mean(rows * rows, axis=-1, keepdims=True) + EPSILON)
    return rows * inverse, inverse


def norm_backward(grad, unit, inverse, gain):
    scaled = grad * gain
    return inverse * (scaled - unit * jnp.mean(scaled * unit, axis=-1, keepdims=True))


def lanes(head):
    return pl.ds(pl.multiple_of(head * HEAD, HEAD), HEAD)


def kernel(
    query_hbm, key_hbm, value_hbm, query_gain_ref, key_gain_ref, segment_ref, grad_hbm,
    attended_hbm, grad_query_hbm, grad_key_hbm, grad_value_hbm, query_gain_hbm,
    key_gain_hbm,
    window, ids, bias, query_norm, grad_rows, grad_cols, key_norm, key_unit, scores, tops, totals, factors,
    corrections, outputs,
    weights, grad_scores, partial, outgoing, incoming,
    query_ref, grad_ref, attended_ref, grad_query_ref, grad_key_ref, grad_value_ref, sums, exchange, gains,
    up_send, up_recv, id_send, id_recv, down_send, down_recv, swap_send, swap_recv, load, wide_store, narrow_store, gain_store,
):
    count = lax.axis_size("seq")
    me = lax.axis_index("seq")
    dp = lax.axis_index("dp")
    after = lax.rem(me + 1, count)
    before = lax.rem(me + count - 1, count)

    place = lax.rem(me, ROW)
    sizes = (lax.axis_size("dp"), count // ROW, 4, 4)
    mine = (dp, me // ROW, lax.rem(place, 4), place // 4)

    def peer(phase, at):
        if phase == 0:
            return at, me
        return dp, me + (at - mine[phase]) * (0, ROW, 1, 4)[phase]

    loads = []
    for head in range(KV):
        at = slice(head * HEAD, (head + 1) * HEAD)
        loads.append((key_hbm.at[:, at], window.at[head, 0, pl.ds(0, TOK)]))
        loads.append((value_hbm.at[:, at], window.at[head, 0, pl.ds(TOK, TOK)]))
    loads.append((query_hbm, query_ref))
    loads.append((grad_hbm, grad_ref))
    loads = [pltpu.make_async_copy(a, b, load.at[i]) for i, (a, b) in enumerate(loads)]
    for copy in loads:
        copy.start()

    barrier = pltpu.get_barrier_semaphore()
    greeted = 2
    for neighbour in (after, before):
        pl.semaphore_signal(barrier, inc=1, device_id=(dp, neighbour), device_id_type=MESH)
    for phase in range(4):
        for j in range(1, sizes[phase]):
            if phase == 3 and j == 2:
                continue
            target = peer(phase, lax.rem(mine[phase] + j, sizes[phase]))
            pl.semaphore_signal(barrier, inc=1, device_id=target, device_id_type=MESH)
            greeted += 1

    def swap(phase, j, slot):
        return pltpu.make_async_remote_copy(
            src_ref=exchange.at[phase, slot],
            dst_ref=exchange.at[phase, slot],
            send_sem=swap_send.at[phase, j],
            recv_sem=swap_recv.at[phase, slot],
            device_id=peer(phase, lax.rem(mine[phase] + j, sizes[phase])),
            device_id_type=MESH,
        )

    def swap_start(phase):
        if phase == 4:
            slot = lax.rem(mine[3] + 3, 4)
            swap(3, 1, slot).start()
            return
        exchange[phase, mine[phase]] = sums[...]
        for j in range(1, sizes[phase]):
            if phase < 3 or j != 2:
                swap(phase, j, mine[phase]).start()

    def swap_finish(phase):
        if phase == 4:
            swap(3, 1, lax.rem(mine[3] + 2, 4)).wait_recv()
            swap(3, 1, lax.rem(mine[3] + 3, 4)).wait_send()
            phase = 3
        else:
            for j in range(1, sizes[phase]):
                if phase < 3 or j != 2:
                    swap(phase, j, lax.rem(mine[phase] + j, sizes[phase])).wait_recv()
                    swap(phase, j, mine[phase]).wait_send()
            if phase == 3:
                return
        total = exchange[phase, 0]
        for slot in range(1, sizes[phase]):
            total = total + exchange[phase, slot]
        sums[...] = total

    def up(head, step, part):
        rows = pl.ds(part * TOK, TOK)
        return pltpu.make_async_remote_copy(
            src_ref=window.at[head, step, rows],
            dst_ref=window.at[head, step + 1, rows],
            send_sem=up_send.at[head, step, part],
            recv_sem=up_recv.at[head, step, part],
            device_id=(dp, after),
            device_id_type=MESH,
        )

    def up_ids(step):
        return pltpu.make_async_remote_copy(
            src_ref=ids.at[step],
            dst_ref=ids.at[step + 1],
            send_sem=id_send.at[step],
            recv_sem=id_recv.at[step],
            device_id=(dp, after),
            device_id_type=MESH,
        )

    def down(head, step, part):
        rows = pl.ds(part * TOK, TOK)
        return pltpu.make_async_remote_copy(
            src_ref=outgoing.at[head, step, rows],
            dst_ref=incoming.at[head, step, rows],
            send_sem=down_send.at[head, step, part],
            recv_sem=down_recv.at[head, step, part],
            device_id=(dp, before),
            device_id_type=MESH,
        )

    own_ids = segment_ref[...].astype(jnp.float32)
    ids[0] = jnp.broadcast_to(own_ids, (16, TOK)).astype(jnp.bfloat16)
    def prepare(head):
        group, member = head // GROUP, lax.rem(head, GROUP)
        rows = pl.ds(pl.multiple_of(member * TOK, TOK), TOK)
        unit, _ = normalize(query_ref[:, lanes(head)].astype(jnp.float32))
        query_norm[group, rows, :] = (unit * query_gain_ref[...]).astype(jnp.bfloat16)
        grad = grad_ref[:, lanes(head)]
        grad_rows[group, rows, :] = grad
        grad_cols[group, :, rows] = grad.astype(jnp.float32).T.astype(jnp.bfloat16)

    def mask_block(step):
        key_ids = jnp.broadcast_to(ids[step, 0:16, :].astype(jnp.float32)[0:1], (TOK, TOK)).T
        seen = key_ids == own_ids
        key_at = lax.broadcasted_iota(jnp.int32, (TOK, TOK), 0)
        query_at = lax.broadcasted_iota(jnp.int32, (TOK, TOK), 1)
        seen = seen & (key_at <= query_at + jnp.where(step > 0, TOK, 0))
        bias[step] = jnp.where(seen, 0.0, -1e30)

    def score_block(head, step):
        unit, _ = normalize(window[head, step, :TOK].astype(jnp.float32))
        key_unit[head, step] = unit
        keys = (unit * key_gain_ref[...]).astype(jnp.bfloat16)
        key_norm[head, step] = keys
        raw = dot(keys, query_norm[head], NT) * (SCALE * math.log2(math.e))
        block_bias = bias[step]
        for member in range(GROUP):
            at = slice(member * TOK, (member + 1) * TOK)
            part = raw[:, at] + block_bias
            top = jnp.max(part, axis=0, keepdims=True)
            part = jnp.exp2(part - top)
            scores[head, step, :, at] = part
            tops[head, step, :, at] = top
            totals[head, step, :, at] = jnp.sum(part, axis=0, keepdims=True)

    near, rows = SPAN * TOK, BLOCKS * TOK

    def weigh_block(head):
        top = jnp.max(tops[head], axis=0, keepdims=True)
        factor = jnp.exp2(tops[head] - top)
        factor = factor / jnp.sum(factor * totals[head], axis=0, keepdims=True)
        factors[head] = factor
        at = lax.rem(head, 2)
        weights[at, near:] = (scores[head, SPAN] * factor[SPAN]).astype(jnp.bfloat16)
        grad_value = dot(weights[at, near:], grad_rows[head], NN)
        outgoing[head, 0, TOK:] = grad_value.astype(jnp.bfloat16)
        down(head, 0, 1).start()

    def attend(head):
        at = lax.rem(head, 2)
        weights[at, :near] = (
            (scores[head, :SPAN] * factors[head, :SPAN]).reshape(near, WIDTH).astype(jnp.bfloat16)
        )
        output = dot(window[head, :, TOK:].reshape(rows, HEAD), weights[at], TN)
        output = output.astype(jnp.bfloat16)
        outputs[at] = output
        correction = jnp.sum(
            output.astype(jnp.float32) * grad_cols[head].astype(jnp.float32), axis=0, keepdims=True
        )
        corrections[head] = correction
        grad_prob = dot(window[head, SPAN, TOK:], grad_rows[head], NT)
        grad_scores[at, near:] = (
            scores[head, SPAN] * (factors[head, SPAN] * SCALE) * (grad_prob - correction)
        ).astype(jnp.bfloat16)
        grad_key = dot(grad_scores[at, near:], query_norm[head], NN)
        outgoing[head, 0, :TOK] = grad_key.astype(jnp.bfloat16)
        down(head, 0, 0).start()
        sums[8:] += jnp.sum((grad_key * key_unit[head, SPAN]).reshape(-1, 8, HEAD), axis=0)

    def head_rest(head):
        at = lax.rem(head, 2)
        grad_value = dot(weights[at, :near], grad_rows[head], NN)
        partial[head, :, TOK:] = grad_value.reshape(SPAN, TOK, HEAD)
        value_rows = window[head, :SPAN, TOK:].reshape(near, HEAD)
        grad_prob = dot(value_rows, grad_rows[head], NT)
        scaled = (scores[head, :SPAN] * (factors[head, :SPAN] * SCALE)).reshape(near, WIDTH)
        grad_scores[at, :near] = (scaled * (grad_prob - corrections[head])).astype(jnp.bfloat16)
        grad_key = dot(grad_scores[at, :near], query_norm[head], NN)
        partial[head, :, :TOK] = grad_key.reshape(SPAN, TOK, HEAD)
        units = key_unit[head, :SPAN].reshape(near, HEAD)
        sums[8:] += jnp.sum((grad_key * units).reshape(-1, 8, HEAD), axis=0)
        output = outputs[at].astype(jnp.float32)

        for member in range(GROUP):
            cols = slice(member * TOK, (member + 1) * TOK)
            attended_ref[:, lanes(head * GROUP + member)] = output[:, cols].T.astype(jnp.bfloat16)
        grad_query = dot(key_norm[head].reshape(rows, HEAD), grad_scores[at], TN)
        for member in range(GROUP):
            cols = slice(member * TOK, (member + 1) * TOK)
            where = lanes(head * GROUP + member)
            unit, query_inverse = normalize(query_ref[:, where].astype(jnp.float32))
            grad = grad_query[:, cols].T
            sums[:8] += jnp.sum((grad * unit).reshape(TOK // 8, 8, HEAD), axis=0)
            grad_query_ref[:, where] = norm_backward(
                grad, unit, query_inverse, query_gain_ref[...]
            ).astype(jnp.bfloat16)

    def narrow(head, part):
        at = pl.ds(head * HEAD, HEAD)
        source = (grad_key_ref, grad_value_ref)[part]
        target = (grad_key_hbm, grad_value_hbm)[part]
        return pltpu.make_async_copy(
            source.at[:, at], target.at[:, at], narrow_store.at[head, part]
        )

    def wide(head, part):
        at = pl.ds(pl.multiple_of(head * GROUP * HEAD, HEAD), GROUP * HEAD)
        source = (attended_ref, grad_query_ref)[part]
        target = (attended_hbm, grad_query_hbm)[part]
        return pltpu.make_async_copy(
            source.at[:, at], target.at[:, at], wide_store.at[head, part]
        )

    def receive_up(head, step, part):
        @pl.when((step >= 0) & (step <= SPAN))
        def _():
            if head == 0 and part == 0:

                @pl.when(step > 0)
                def _():
                    up_ids(step - 1).wait_recv()

                @pl.when(step < SPAN)
                def _():
                    up_ids(step).start()

            @pl.when(step > 0)
            def _():
                up(head, step - 1, part).wait_recv()

            @pl.when(step < SPAN)
            def _():
                up(head, step, part).start()

    def receive_down(head, back, part):
        rows = slice(part * TOK, (part + 1) * TOK)

        @pl.when((back >= 1) & (back <= SPAN))
        def _():
            down(head, back - 1, part).wait_recv()
            total = incoming[head, back - 1, rows].astype(jnp.float32)
            total = total + partial[head, SPAN - back, rows]

            @pl.when(back < SPAN)
            def _():
                outgoing[head, back, rows] = total.astype(jnp.bfloat16)
                down(head, back, part).start()

            @pl.when(back == SPAN)
            def _():
                at = slice(head * HEAD, (head + 1) * HEAD)
                if part == 1:
                    grad_value_ref[:, at] = total.astype(jnp.bfloat16)
                else:
                    unit, inverse = normalize(window[head, 0, :TOK].astype(jnp.float32))
                    grad_key_ref[:, at] = norm_backward(
                        total, unit, inverse, key_gain_ref[...]
                    ).astype(jnp.bfloat16)
                narrow(head, part).start()

    def work(head, step):
        @pl.when((step >= 1) & (step <= SPAN))
        def _():
            @pl.when(head == 0)
            def _():
                mask_block(step)

            score_block(head, step)

    def whole(head):
        head_rest(head)
        wide(head, 0).start()
        wide(head, 1).start()

    sums[...] = jnp.zeros(sums.shape, jnp.float32)
    for copy in loads[:-2]:
        copy.wait()
    pl.semaphore_wait(barrier, greeted)

    def ready(head):
        def one(member, carry):
            prepare(head * GROUP + member)
            return carry

        @pl.when(head == 0)
        def _():
            for copy in loads[-2:]:
                copy.wait()
            mask_block(0)

        lax.fori_loop(0, GROUP, one, 0)
        score_block(head, 0)

    def offset(head):
        return sum(
            jnp.where(head >= k, OFFSETS[k] - OFFSETS[k - 1], 0) for k in range(1, KV)
        )

    def one_round(index, carry):
        for place_in_pair in range(2):
            for part in range(2):
                for head in (place_in_pair + 2, place_in_pair):
                    step = index - OFFSETS[head]
                    receive_up(head, step, part)
                    receive_down(head, step - SPAN - LATE[head], 1 - part)

        def second(head, inner):
            work(head, index - offset(head))
            return inner

        @pl.when(index < KV)
        def _():
            ready(index)

        lax.fori_loop(0, KV, second, 0)
        for stage, late in ((weigh_block, 0), (attend, 0), (whole, LATE[0])):

            def third(head, inner, stage=stage, late=late):
                @pl.when(index == offset(head) + SPAN + jnp.where(head < 2, late, 0))
                def _():
                    stage(head)

                return inner

            lax.fori_loop(0, KV, third, 0)


        for phase in range(6):

            @pl.when(index == TAIL + SWAPS[phase])
            def _():
                if phase > 0:
                    swap_finish(phase - 1)
                if phase < 5:
                    swap_start(phase)

        return carry

    lax.fori_loop(0, ROUNDS, one_round, 0)

    def drain(head, carry):
        def one(step, inner):
            for part in range(2):
                up(head, step, part).wait_send()
                down(head, step, part).wait_send()

            @pl.when(head == 0)
            def _():
                up_ids(step).wait_send()

            return inner

        return lax.fori_loop(0, SPAN, one, carry)

    lax.fori_loop(0, KV, drain, 0)
    for head in range(KV):
        for part in range(2):
            wide(head, part).wait()
            narrow(head, part).wait()
    for part, target in enumerate((query_gain_hbm, key_gain_hbm)):
        gains[part] = jnp.sum(sums[part * 8 : part * 8 + 8], axis=0, keepdims=True)
        pltpu.make_async_copy(gains.at[part], target, gain_store.at[part]).start()
    for part, target in enumerate((query_gain_hbm, key_gain_hbm)):
        pltpu.make_async_copy(gains.at[part], target, gain_store.at[part]).wait()


def deliver(*refs):
    loads, stores = [], []
    for i in range(6):
        source, target, held = refs[i], refs[6 + i], refs[12 + i]
        loads.append(pltpu.make_async_copy(source, held, refs[18].at[i]))
        stores.append(pltpu.make_async_copy(held, target, refs[19].at[i]))
    for copy in loads:
        copy.start()
    for load, store in zip(loads, stores):
        load.wait()
        store.start()
    for copy in stores:
        copy.wait()


def local(query_raw, key_raw, values, query_gain, key_gain, segment_ids, grad_attended):
    wide, narrow = (TOK, KV * GROUP * HEAD), (TOK, KV * HEAD)
    vmem = pl.BlockSpec(memory_space=pltpu.VMEM)
    hbm = pl.BlockSpec(memory_space=pltpu.HBM)
    dma = pltpu.SemaphoreType.DMA
    outs_like = (
        jax.ShapeDtypeStruct(wide, jnp.bfloat16),
        jax.ShapeDtypeStruct(wide, jnp.bfloat16),
        jax.ShapeDtypeStruct(narrow, jnp.bfloat16),
        jax.ShapeDtypeStruct(narrow, jnp.bfloat16),
    ) + (jax.ShapeDtypeStruct((1, HEAD), jnp.float32),) * 2
    outs = pl.pallas_call(
        kernel,
        out_shape=outs_like,
        in_specs=[hbm, hbm, hbm, vmem, vmem, vmem, hbm],
        out_specs=(hbm,) * 6,
        scratch_shapes=[
            pltpu.VMEM((KV, BLOCKS, 2 * TOK, HEAD), jnp.bfloat16),
            pltpu.VMEM((BLOCKS, 16, TOK), jnp.bfloat16),
            pltpu.VMEM((BLOCKS, TOK, TOK), jnp.float32),
            pltpu.VMEM((KV, WIDTH, HEAD), jnp.bfloat16),
            pltpu.VMEM((KV, WIDTH, HEAD), jnp.bfloat16),
            pltpu.VMEM((KV, HEAD, WIDTH), jnp.bfloat16),
            pltpu.VMEM((KV, BLOCKS, TOK, HEAD), jnp.bfloat16),
            pltpu.VMEM((KV, BLOCKS, TOK, HEAD), jnp.float32),
            pltpu.VMEM((KV, BLOCKS, TOK, WIDTH), jnp.float32),
            pltpu.VMEM((KV, BLOCKS, 1, WIDTH), jnp.float32),
            pltpu.VMEM((KV, BLOCKS, 1, WIDTH), jnp.float32),
            pltpu.VMEM((KV, BLOCKS, 1, WIDTH), jnp.float32),
            pltpu.VMEM((KV, 1, WIDTH), jnp.float32),
            pltpu.VMEM((2, HEAD, WIDTH), jnp.bfloat16),
            pltpu.VMEM((2, BLOCKS * TOK, WIDTH), jnp.bfloat16),
            pltpu.VMEM((2, BLOCKS * TOK, WIDTH), jnp.bfloat16),
            pltpu.VMEM((KV, SPAN, 2 * TOK, HEAD), jnp.float32),
            pltpu.VMEM((KV, SPAN, 2 * TOK, HEAD), jnp.bfloat16),
            pltpu.VMEM((KV, SPAN, 2 * TOK, HEAD), jnp.bfloat16),
            pltpu.VMEM(wide, jnp.bfloat16),
            pltpu.VMEM(wide, jnp.bfloat16),
            pltpu.VMEM(wide, jnp.bfloat16),
            pltpu.VMEM(wide, jnp.bfloat16),
            pltpu.VMEM(narrow, jnp.bfloat16),
            pltpu.VMEM(narrow, jnp.bfloat16),
            pltpu.VMEM((16, HEAD), jnp.float32),
            pltpu.VMEM((4, 8, 16, HEAD), jnp.float32),
            pltpu.VMEM((2, 1, HEAD), jnp.float32),
            dma((KV, SPAN, 2)),
            dma((KV, SPAN, 2)),
            dma((SPAN,)),
            dma((SPAN,)),
            dma((KV, SPAN, 2)),
            dma((KV, SPAN, 2)),
            dma((4, 8)),
            dma((4, 8)),
            dma((2 * KV + 2,)),
            dma((KV, 2)),
            dma((KV, 2)),
            dma((2,)),
        ],
        compiler_params=pltpu.CompilerParams(
            collective_id=0, has_side_effects=True, vmem_limit_bytes=LIMIT << 20
        ),
        cost_estimate=pl.CostEstimate(
            flops=2 * 6 * TOK * BLOCKS * TOK * HEAD * KV * GROUP,
            bytes_accessed=3 << 20,
            transcendentals=TOK * BLOCKS * TOK * KV * GROUP,
        ),
        name="attention",
    )(
        query_raw[0],
        key_raw[0],
        values[0],
        query_gain[None],
        key_gain[None],
        segment_ids,
        grad_attended[0],
    )
    attended, grad_query, grad_key, grad_values, grad_query_gain, grad_key_gain = pl.pallas_call(
        deliver,
        out_shape=outs_like,
        in_specs=[hbm] * 6,
        out_specs=(hbm,) * 6,
        scratch_shapes=[pltpu.VMEM(like.shape, like.dtype) for like in outs_like]
        + [dma((6,)), dma((6,))],
        name="deliver",
    )(*outs)
    return (
        attended[None],
        grad_query[None],
        grad_key[None],
        grad_values[None],
        grad_query_gain[0],
        grad_key_gain[0],
    )


def solution(mesh):
    row = P("dp", "seq", None)
    return jax.shard_map(
        local,
        mesh=mesh,
        in_specs=(row, row, row, P(), P(), P("dp", "seq"), row),
        out_specs=(row, row, row, row, P(), P()),
        check_vma=False,
    )
```

```python
import math

import jax
import jax.numpy as jnp
from jax import lax
from jax.experimental import pallas as pl
from jax.experimental.pallas import tpu as pltpu
from jax.sharding import PartitionSpec as P

SPAN = 7
BLOCKS = SPAN + 1
HEAD = 128
TOK = 128
KV = 4
GROUP = 5
OFFSETS = (0, 0, 7, 7)
LATE = (1, 1, 0, 0)
ROW = 16
WIDTH = GROUP * TOK
ROUNDS = OFFSETS[-1] + 2 * SPAN + 1
TAIL = OFFSETS[-1] + SPAN
SWAPS = (0, 1, 2, 3, 5, 6)
EPSILON = 1e-06
LIMIT = 60
SCALE = HEAD**-0.5
MESH = pl.DeviceIdType.MESH

NT = (((1,), (1,)), ((), ()))
NN = (((1,), (0,)), ((), ()))
TN = (((0,), (0,)), ((), ()))


def dot(a, b, dims):
    return lax.dot_general(a, b, dims, preferred_element_type=jnp.float32)


def normalize(rows):
    inverse = lax.rsqrt(jnp.mean(rows * rows, axis=-1, keepdims=True) + EPSILON)
    return rows * inverse, inverse


def norm_backward(grad, unit, inverse, gain):
    scaled = grad * gain
    return inverse * (scaled - unit * jnp.mean(scaled * unit, axis=-1, keepdims=True))


def lanes(head):
    return pl.ds(pl.multiple_of(head * HEAD, HEAD), HEAD)


def kernel(
    query_hbm, key_hbm, value_hbm, query_gain_ref, key_gain_ref, segment_ref, grad_hbm,
    attended_hbm, grad_query_hbm, grad_key_hbm, grad_value_hbm, query_gain_hbm,
    key_gain_hbm,
    window, ids, bias, query_norm, grad_rows, grad_cols, key_norm, key_unit, scores, tops, totals, factors,
    corrections, outputs,
    weights, grad_scores, partial, outgoing, incoming,
    query_ref, grad_ref, attended_ref, grad_query_ref, grad_key_ref, grad_value_ref, sums, exchange, gains,
    up_send, up_recv, id_send, id_recv, down_send, down_recv, swap_send, swap_recv, load, wide_store, narrow_store, gain_store,
):
    count = lax.axis_size("seq")
    me = lax.axis_index("seq")
    dp = lax.axis_index("dp")
    after = lax.rem(me + 1, count)
    before = lax.rem(me + count - 1, count)

    place = lax.rem(me, ROW)
    sizes = (lax.axis_size("dp"), count // ROW, 4, 4)
    mine = (dp, me // ROW, lax.rem(place, 4), place // 4)

    def peer(phase, at):
        if phase == 0:
            return at, me
        return dp, me + (at - mine[phase]) * (0, ROW, 1, 4)[phase]

    barrier = pltpu.get_barrier_semaphore()
    greeted = 2
    for neighbour in (after, before):
        pl.semaphore_signal(barrier, inc=1, device_id=(dp, neighbour), device_id_type=MESH)
    for phase in range(4):
        for j in range(1, sizes[phase]):
            if phase == 3 and j == 2:
                continue
            target = peer(phase, lax.rem(mine[phase] + j, sizes[phase]))
            pl.semaphore_signal(barrier, inc=1, device_id=target, device_id_type=MESH)
            greeted += 1

    loads = []
    for head in range(KV):
        at = slice(head * HEAD, (head + 1) * HEAD)
        loads.append((key_hbm.at[:, at], window.at[head, 0, pl.ds(0, TOK)]))
        loads.append((value_hbm.at[:, at], window.at[head, 0, pl.ds(TOK, TOK)]))
    loads.append((query_hbm, query_ref))
    loads.append((grad_hbm, grad_ref))
    loads = [pltpu.make_async_copy(a, b, load.at[i]) for i, (a, b) in enumerate(loads)]
    for copy in loads:
        copy.start()

    def swap(phase, j, slot):
        return pltpu.make_async_remote_copy(
            src_ref=exchange.at[phase, slot],
            dst_ref=exchange.at[phase, slot],
            send_sem=swap_send.at[phase, j],
            recv_sem=swap_recv.at[phase, slot],
            device_id=peer(phase, lax.rem(mine[phase] + j, sizes[phase])),
            device_id_type=MESH,
        )

    def swap_start(phase):
        if phase == 4:
            slot = lax.rem(mine[3] + 3, 4)
            swap(3, 1, slot).start()
            return
        exchange[phase, mine[phase]] = sums[...]
        for j in range(1, sizes[phase]):
            if phase < 3 or j != 2:
                swap(phase, j, mine[phase]).start()

    def swap_finish(phase):
        if phase == 4:
            swap(3, 1, lax.rem(mine[3] + 2, 4)).wait_recv()
            swap(3, 1, lax.rem(mine[3] + 3, 4)).wait_send()
            phase = 3
        else:
            for j in range(1, sizes[phase]):
                if phase < 3 or j != 2:
                    swap(phase, j, lax.rem(mine[phase] + j, sizes[phase])).wait_recv()
                    swap(phase, j, mine[phase]).wait_send()
            if phase == 3:
                return
        total = exchange[phase, 0]
        for slot in range(1, sizes[phase]):
            total = total + exchange[phase, slot]
        sums[...] = total

    def up(head, step, part):
        rows = pl.ds(part * TOK, TOK)
        return pltpu.make_async_remote_copy(
            src_ref=window.at[head, step, rows],
            dst_ref=window.at[head, step + 1, rows],
            send_sem=up_send.at[head, step, part],
            recv_sem=up_recv.at[head, step, part],
            device_id=(dp, after),
            device_id_type=MESH,
        )

    def up_ids(step):
        return pltpu.make_async_remote_copy(
            src_ref=ids.at[step],
            dst_ref=ids.at[step + 1],
            send_sem=id_send.at[step],
            recv_sem=id_recv.at[step],
            device_id=(dp, after),
            device_id_type=MESH,
        )

    def down(head, step, part):
        rows = pl.ds(part * TOK, TOK)
        return pltpu.make_async_remote_copy(
            src_ref=outgoing.at[head, step, rows],
            dst_ref=incoming.at[head, step, rows],
            send_sem=down_send.at[head, step, part],
            recv_sem=down_recv.at[head, step, part],
            device_id=(dp, before),
            device_id_type=MESH,
        )

    own_ids = segment_ref[...].astype(jnp.float32)
    ids[0] = jnp.broadcast_to(own_ids, (16, TOK)).astype(jnp.bfloat16)
    def prepare(head):
        group, member = head // GROUP, lax.rem(head, GROUP)
        rows = pl.ds(pl.multiple_of(member * TOK, TOK), TOK)
        unit, _ = normalize(query_ref[:, lanes(head)].astype(jnp.float32))
        query_norm[group, rows, :] = (unit * query_gain_ref[...]).astype(jnp.bfloat16)
        grad = grad_ref[:, lanes(head)]
        grad_rows[group, rows, :] = grad
        grad_cols[group, :, rows] = grad.astype(jnp.float32).T.astype(jnp.bfloat16)

    def mask_block(step):
        key_ids = jnp.broadcast_to(ids[step, 0:16, :].astype(jnp.float32)[0:1], (TOK, TOK)).T
        seen = key_ids == own_ids
        key_at = lax.broadcasted_iota(jnp.int32, (TOK, TOK), 0)
        query_at = lax.broadcasted_iota(jnp.int32, (TOK, TOK), 1)
        seen = seen & (key_at <= query_at + jnp.where(step > 0, TOK, 0))
        bias[step] = jnp.where(seen, 0.0, -1e30)

    def score_block(head, step):
        unit, _ = normalize(window[head, step, :TOK].astype(jnp.float32))
        key_unit[head, step] = unit
        keys = (unit * key_gain_ref[...]).astype(jnp.bfloat16)
        key_norm[head, step] = keys
        raw = dot(keys, query_norm[head], NT) * (SCALE * math.log2(math.e))
        block_bias = bias[step]
        for member in range(GROUP):
            at = slice(member * TOK, (member + 1) * TOK)
            part = raw[:, at] + block_bias
            top = jnp.max(part, axis=0, keepdims=True)
            part = jnp.exp2(part - top)
            scores[head, step, :, at] = part
            tops[head, step, :, at] = top
            totals[head, step, :, at] = jnp.sum(part, axis=0, keepdims=True)

    near, rows = SPAN * TOK, BLOCKS * TOK

    def weigh_block(head):
        top = jnp.max(tops[head], axis=0, keepdims=True)
        factor = jnp.exp2(tops[head] - top)
        factor = factor / jnp.sum(factor * totals[head], axis=0, keepdims=True)
        factors[head] = factor
        at = lax.rem(head, 2)
        weights[at, near:] = (scores[head, SPAN] * factor[SPAN]).astype(jnp.bfloat16)
        grad_value = dot(weights[at, near:], grad_rows[head], NN)
        outgoing[head, 0, TOK:] = grad_value.astype(jnp.bfloat16)
        down(head, 0, 1).start()

    def attend(head):
        at = lax.rem(head, 2)
        weights[at, :near] = (
            (scores[head, :SPAN] * factors[head, :SPAN]).reshape(near, WIDTH).astype(jnp.bfloat16)
        )
        output = dot(window[head, :, TOK:].reshape(rows, HEAD), weights[at], TN)
        output = output.astype(jnp.bfloat16)
        outputs[at] = output
        correction = jnp.sum(
            output.astype(jnp.float32) * grad_cols[head].astype(jnp.float32), axis=0, keepdims=True
        )
        corrections[head] = correction
        grad_prob = dot(window[head, SPAN, TOK:], grad_rows[head], NT)
        grad_scores[at, near:] = (
            scores[head, SPAN] * (factors[head, SPAN] * SCALE) * (grad_prob - correction)
        ).astype(jnp.bfloat16)
        grad_key = dot(grad_scores[at, near:], query_norm[head], NN)
        outgoing[head, 0, :TOK] = grad_key.astype(jnp.bfloat16)
        down(head, 0, 0).start()
        sums[8:] += jnp.sum((grad_key * key_unit[head, SPAN]).reshape(-1, 8, HEAD), axis=0)

    def head_rest(head):
        at = lax.rem(head, 2)
        grad_value = dot(weights[at, :near], grad_rows[head], NN)
        partial[head, :, TOK:] = grad_value.reshape(SPAN, TOK, HEAD)
        value_rows = window[head, :SPAN, TOK:].reshape(near, HEAD)
        grad_prob = dot(value_rows, grad_rows[head], NT)
        scaled = (scores[head, :SPAN] * (factors[head, :SPAN] * SCALE)).reshape(near, WIDTH)
        grad_scores[at, :near] = (scaled * (grad_prob - corrections[head])).astype(jnp.bfloat16)
        grad_key = dot(grad_scores[at, :near], query_norm[head], NN)
        partial[head, :, :TOK] = grad_key.reshape(SPAN, TOK, HEAD)
        units = key_unit[head, :SPAN].reshape(near, HEAD)
        sums[8:] += jnp.sum((grad_key * units).reshape(-1, 8, HEAD), axis=0)
        output = outputs[at].astype(jnp.float32)

        for member in range(GROUP):
            cols = slice(member * TOK, (member + 1) * TOK)
            attended_ref[:, lanes(head * GROUP + member)] = output[:, cols].T.astype(jnp.bfloat16)
        grad_query = dot(key_norm[head].reshape(rows, HEAD), grad_scores[at], TN)
        for member in range(GROUP):
            cols = slice(member * TOK, (member + 1) * TOK)
            where = lanes(head * GROUP + member)
            unit, query_inverse = normalize(query_ref[:, where].astype(jnp.float32))
            grad = grad_query[:, cols].T
            sums[:8] += jnp.sum((grad * unit).reshape(TOK // 8, 8, HEAD), axis=0)
            grad_query_ref[:, where] = norm_backward(
                grad, unit, query_inverse, query_gain_ref[...]
            ).astype(jnp.bfloat16)

    def narrow(head, part):
        at = pl.ds(head * HEAD, HEAD)
        source = (grad_key_ref, grad_value_ref)[part]
        target = (grad_key_hbm, grad_value_hbm)[part]
        return pltpu.make_async_copy(
            source.at[:, at], target.at[:, at], narrow_store.at[head, part]
        )

    def wide(head, part):
        at = pl.ds(pl.multiple_of(head * GROUP * HEAD, HEAD), GROUP * HEAD)
        source = (attended_ref, grad_query_ref)[part]
        target = (attended_hbm, grad_query_hbm)[part]
        return pltpu.make_async_copy(
            source.at[:, at], target.at[:, at], wide_store.at[head, part]
        )

    def receive_up(head, step, part):
        @pl.when((step >= 0) & (step <= SPAN))
        def _():
            if head == 0 and part == 0:

                @pl.when(step > 0)
                def _():
                    up_ids(step - 1).wait_recv()

                @pl.when(step < SPAN)
                def _():
                    up_ids(step).start()

            @pl.when(step > 0)
            def _():
                up(head, step - 1, part).wait_recv()

            @pl.when(step < SPAN)
            def _():
                up(head, step, part).start()

    def receive_down(head, back, part):
        rows = slice(part * TOK, (part + 1) * TOK)

        @pl.when((back >= 1) & (back <= SPAN))
        def _():
            down(head, back - 1, part).wait_recv()
            total = incoming[head, back - 1, rows].astype(jnp.float32)
            total = total + partial[head, SPAN - back, rows]

            @pl.when(back < SPAN)
            def _():
                outgoing[head, back, rows] = total.astype(jnp.bfloat16)
                down(head, back, part).start()

            @pl.when(back == SPAN)
            def _():
                at = slice(head * HEAD, (head + 1) * HEAD)
                if part == 1:
                    grad_value_ref[:, at] = total.astype(jnp.bfloat16)
                else:
                    unit, inverse = normalize(window[head, 0, :TOK].astype(jnp.float32))
                    grad_key_ref[:, at] = norm_backward(
                        total, unit, inverse, key_gain_ref[...]
                    ).astype(jnp.bfloat16)
                narrow(head, part).start()

    def work(head, step):
        @pl.when((step >= 1) & (step <= SPAN))
        def _():
            @pl.when(head == 0)
            def _():
                mask_block(step)

            score_block(head, step)

    def whole(head):
        head_rest(head)
        wide(head, 0).start()
        wide(head, 1).start()

    sums[...] = jnp.zeros(sums.shape, jnp.float32)
    for copy in loads[:-2]:
        copy.wait()

    def ready(head):
        def one(member, carry):
            prepare(head * GROUP + member)
            return carry

        @pl.when(head == 0)
        def _():
            for copy in loads[-2:]:
                copy.wait()
            mask_block(0)

        lax.fori_loop(0, GROUP, one, 0)
        score_block(head, 0)

    ready(0)
    pl.semaphore_wait(barrier, greeted)

    def offset(head):
        return sum(
            jnp.where(head >= k, OFFSETS[k] - OFFSETS[k - 1], 0) for k in range(1, KV)
        )

    def one_round(index, carry):
        for place_in_pair in range(2):
            for part in range(2):
                for head in (place_in_pair + 2, place_in_pair):
                    step = index - OFFSETS[head]
                    receive_up(head, step, part)
                    receive_down(head, step - SPAN - LATE[head], 1 - part)

        def second(head, inner):
            work(head, index - offset(head))
            return inner

        @pl.when(index < KV - 1)
        def _():
            ready(index + 1)

        lax.fori_loop(0, KV, second, 0)
        for stage, late in ((weigh_block, 0), (attend, 0), (whole, LATE[0])):

            def third(head, inner, stage=stage, late=late):
                @pl.when(index == offset(head) + SPAN + jnp.where(head < 2, late, 0))
                def _():
                    stage(head)

                return inner

            lax.fori_loop(0, KV, third, 0)


        for phase in range(6):

            @pl.when(index == TAIL + SWAPS[phase])
            def _():
                if phase > 0:
                    swap_finish(phase - 1)
                if phase < 5:
                    swap_start(phase)

        return carry

    lax.fori_loop(0, ROUNDS, one_round, 0)

    def drain(head, carry):
        def one(step, inner):
            for part in range(2):
                up(head, step, part).wait_send()
                down(head, step, part).wait_send()

            @pl.when(head == 0)
            def _():
                up_ids(step).wait_send()

            return inner

        return lax.fori_loop(0, SPAN, one, carry)

    lax.fori_loop(0, KV, drain, 0)
    for head in range(KV):
        for part in range(2):
            wide(head, part).wait()
            narrow(head, part).wait()
    for part, target in enumerate((query_gain_hbm, key_gain_hbm)):
        gains[part] = jnp.sum(sums[part * 8 : part * 8 + 8], axis=0, keepdims=True)
        pltpu.make_async_copy(gains.at[part], target, gain_store.at[part]).start()
    for part, target in enumerate((query_gain_hbm, key_gain_hbm)):
        pltpu.make_async_copy(gains.at[part], target, gain_store.at[part]).wait()


def deliver(*refs):
    loads, stores = [], []
    for i in range(6):
        source, target, held = refs[i], refs[6 + i], refs[12 + i]
        loads.append(pltpu.make_async_copy(source, held, refs[18].at[i]))
        stores.append(pltpu.make_async_copy(held, target, refs[19].at[i]))
    for copy in loads:
        copy.start()
    for load, store in zip(loads, stores):
        load.wait()
        store.start()
    for copy in stores:
        copy.wait()


def local(query_raw, key_raw, values, query_gain, key_gain, segment_ids, grad_attended):
    wide, narrow = (TOK, KV * GROUP * HEAD), (TOK, KV * HEAD)
    vmem = pl.BlockSpec(memory_space=pltpu.VMEM)
    hbm = pl.BlockSpec(memory_space=pltpu.HBM)
    dma = pltpu.SemaphoreType.DMA
    outs_like = (
        jax.ShapeDtypeStruct(wide, jnp.bfloat16),
        jax.ShapeDtypeStruct(wide, jnp.bfloat16),
        jax.ShapeDtypeStruct(narrow, jnp.bfloat16),
        jax.ShapeDtypeStruct(narrow, jnp.bfloat16),
    ) + (jax.ShapeDtypeStruct((1, HEAD), jnp.float32),) * 2
    outs = pl.pallas_call(
        kernel,
        out_shape=outs_like,
        in_specs=[hbm, hbm, hbm, vmem, vmem, vmem, hbm],
        out_specs=(hbm,) * 6,
        scratch_shapes=[
            pltpu.VMEM((KV, BLOCKS, 2 * TOK, HEAD), jnp.bfloat16),
            pltpu.VMEM((BLOCKS, 16, TOK), jnp.bfloat16),
            pltpu.VMEM((BLOCKS, TOK, TOK), jnp.float32),
            pltpu.VMEM((KV, WIDTH, HEAD), jnp.bfloat16),
            pltpu.VMEM((KV, WIDTH, HEAD), jnp.bfloat16),
            pltpu.VMEM((KV, HEAD, WIDTH), jnp.bfloat16),
            pltpu.VMEM((KV, BLOCKS, TOK, HEAD), jnp.bfloat16),
            pltpu.VMEM((KV, BLOCKS, TOK, HEAD), jnp.float32),
            pltpu.VMEM((KV, BLOCKS, TOK, WIDTH), jnp.float32),
            pltpu.VMEM((KV, BLOCKS, 1, WIDTH), jnp.float32),
            pltpu.VMEM((KV, BLOCKS, 1, WIDTH), jnp.float32),
            pltpu.VMEM((KV, BLOCKS, 1, WIDTH), jnp.float32),
            pltpu.VMEM((KV, 1, WIDTH), jnp.float32),
            pltpu.VMEM((2, HEAD, WIDTH), jnp.bfloat16),
            pltpu.VMEM((2, BLOCKS * TOK, WIDTH), jnp.bfloat16),
            pltpu.VMEM((2, BLOCKS * TOK, WIDTH), jnp.bfloat16),
            pltpu.VMEM((KV, SPAN, 2 * TOK, HEAD), jnp.float32),
            pltpu.VMEM((KV, SPAN, 2 * TOK, HEAD), jnp.bfloat16),
            pltpu.VMEM((KV, SPAN, 2 * TOK, HEAD), jnp.bfloat16),
            pltpu.VMEM(wide, jnp.bfloat16),
            pltpu.VMEM(wide, jnp.bfloat16),
            pltpu.VMEM(wide, jnp.bfloat16),
            pltpu.VMEM(wide, jnp.bfloat16),
            pltpu.VMEM(narrow, jnp.bfloat16),
            pltpu.VMEM(narrow, jnp.bfloat16),
            pltpu.VMEM((16, HEAD), jnp.float32),
            pltpu.VMEM((4, 8, 16, HEAD), jnp.float32),
            pltpu.VMEM((2, 1, HEAD), jnp.float32),
            dma((KV, SPAN, 2)),
            dma((KV, SPAN, 2)),
            dma((SPAN,)),
            dma((SPAN,)),
            dma((KV, SPAN, 2)),
            dma((KV, SPAN, 2)),
            dma((4, 8)),
            dma((4, 8)),
            dma((2 * KV + 2,)),
            dma((KV, 2)),
            dma((KV, 2)),
            dma((2,)),
        ],
        compiler_params=pltpu.CompilerParams(
            collective_id=0, has_side_effects=True, vmem_limit_bytes=LIMIT << 20
        ),
        cost_estimate=pl.CostEstimate(
            flops=2 * 6 * TOK * BLOCKS * TOK * HEAD * KV * GROUP,
            bytes_accessed=3 << 20,
            transcendentals=TOK * BLOCKS * TOK * KV * GROUP,
        ),
        name="attention",
    )(
        query_raw[0],
        key_raw[0],
        values[0],
        query_gain[None],
        key_gain[None],
        segment_ids,
        grad_attended[0],
    )
    attended, grad_query, grad_key, grad_values, grad_query_gain, grad_key_gain = pl.pallas_call(
        deliver,
        out_shape=outs_like,
        in_specs=[hbm] * 6,
        out_specs=(hbm,) * 6,
        scratch_shapes=[pltpu.VMEM(like.shape, like.dtype) for like in outs_like]
        + [dma((6,)), dma((6,))],
        name="deliver",
    )(*outs)
    return (
        attended[None],
        grad_query[None],
        grad_key[None],
        grad_values[None],
        grad_query_gain[0],
        grad_key_gain[0],
    )


def solution(mesh):
    row = P("dp", "seq", None)
    return jax.shard_map(
        local,
        mesh=mesh,
        in_specs=(row, row, row, P(), P(), P("dp", "seq"), row),
        out_specs=(row, row, row, row, P(), P()),
        check_vma=False,
    )
```
